32 devices in a mesh: wide: 8 (over z, y), narrow: 4 (over x, core).
Axes of the slice: x: 2, y: 2, z: 4, core: 2. Of those that a mesh axis runs over, the one named last changes fastest.
Arguments:
- points: bfloat16 [256, 256, 256], P('wide', 'narrow'), may hold values from -6 to 6
- targets: bfloat16 [256, 256, 256], P('wide', 'narrow'), may hold values from -6 to 6
- centroids: float32 [128, 256], P('wide'), may hold values from -3 to 3
- block_list: int32 [256], P('wide'), may hold values from 0 to 15
- lengths: int32 [256], P('wide'), may hold values from 1 to 256
- sources: int32 [256], P('wide'), may hold values from 0 to 255, as said below
Outputs:
- rotated: bfloat16 [256, 256, 256], P('wide', 'narrow')
The draws below stay inside these ranges and needn't reach their ends.
Inputs may be any that keep to these rules, and one draw needn't show every extreme that they name: For every index w of wide and slot j below 2, sources[w * 32 + j] = u * 32 + j for some index u of wide, each such input block named exactly once; every other entry names its own position.
All inputs are finite; a program needn't handle non-finite values.
Results may differ from the reference program's by a relative error of at most 0.0051.
Values may be sent and summed in bfloat16 or wider, within the bound.
No kernel may reach another device: no remote copies, remote signals or barrier semaphores. Data moves between devices by JAX's collectives and lax.ppermute only.
A program may use at most 64 MiB of HBM per device.

```python
import math
import jax
import jax.numpy as jnp
import numpy as np
from jax import lax

D = 256
LIST_DEV = 16
BLK = 256
BLK_DEV = 32
MOVE = 2
ITERS = 5
NBLK = 256
LISTS = 128


def draw_sources(key, part):
    groups = NBLK // BLK_DEV
    table = jnp.arange(NBLK, dtype=jnp.int32).reshape(groups, BLK_DEV)
    for slot_index in range(MOVE):
        donors = jax.random.permutation(jax.random.fold_in(key, 17 + slot_index), groups).astype(jnp.int32)
        table = table.at[:, slot_index].set(donors * BLK_DEV + slot_index)
    return table.reshape(NBLK)


def with_ends(drawn, stream_key, least, high):
    longest = drawn.shape.index(max(drawn.shape))
    spots = []
    for shift in (0, 1):
        where = [jax.random.randint(jax.random.fold_in(stream_key, axis), (), 0, length) for axis, length in enumerate(drawn.shape)]
        where[longest] = (where[longest] + shift) % drawn.shape[longest]
        spots.append(tuple(where))
    return drawn.at[spots[0]].set(least).at[spots[1]].set(high)


def block_levels(stream_key, shape, pieces, least, top_value):
    level, own = 1.0, jax.random.fold_in(stream_key, 6)
    for axis_at, parts in pieces:
        heights = jnp.exp(jax.random.uniform(jax.random.fold_in(own, axis_at), (parts,), jnp.float32, least / len(pieces), top_value / len(pieces)))
        level = level * jnp.repeat(heights, shape[axis_at] // parts).reshape([-1 if axis == axis_at else 1 for axis in range(len(shape))])
    return level


def cumulative_ranks(count, slope):
    portions = [(1 << 20) // math.isqrt(standing ** slope) + 1 for standing in range(1, count + 1)]
    width = 1 + sum(portions) // (1 << 30)
    return np.cumsum(np.array([max(1, weight // width) for weight in portions]))


def skewed_ids(key, extent, amount, skew):
    table = cumulative_ranks(amount, skew)
    ticket = jax.random.randint(jax.random.fold_in(key, 1), extent, 0, int(table[amount - 1]))
    standing = jnp.searchsorted(jnp.asarray(table, jnp.int32), ticket, side="right")
    return jax.random.permutation(jax.random.fold_in(key, 2), amount)[standing].astype(jnp.int32)


def centred(key, extent, spread, reach, split=(), held_as=jnp.bfloat16):
    result = jax.random.normal(key, extent, jnp.float32) * spread
    if len(split) > 0:
        result = block_levels(key, extent, split, -0.22, 0.18) * result
    return jnp.clip(result, min=-reach, max=reach).astype(held_as)


def setup_inputs(seed: int = 0) -> dict:
    splits = jax.random.split(jax.random.key(seed), 7)
    points = centred(splits[0], (NBLK, BLK, D), 1.0, 6.0, ((0, 8), (1, 4)))
    targets = centred(splits[1], (NBLK, BLK, D), 1.0, 6.0, ((0, 8), (1, 4)))
    centroids = centred(splits[2], (LISTS, D), 0.5, 3.0, ((0, 8),), jnp.float32)
    block_list = with_ends(skewed_ids(splits[3], (NBLK,), LIST_DEV, 2), jax.random.fold_in(splits[3], 3), 0, LIST_DEV - 1).astype(jnp.int32)
    lengths = with_ends(jax.random.randint(splits[4], (NBLK,), 1, BLK + 1), jax.random.fold_in(splits[4], 1), 1, BLK).astype(jnp.int32)
    sources = draw_sources(jax.random.fold_in(splits[6], 71), 0)
    return dict(points=points, targets=targets, centroids=centroids, block_list=block_list, lengths=lengths, sources=sources)


highest_prec = lax.Precision.HIGHEST

def newton_polar(cross_gram):
    frob_norm = jnp.sqrt(lax.optimization_barrier(jnp.sum(cross_gram * cross_gram, axis=(1, 2), keepdims=True)) + 1e-06)
    polar_iter = cross_gram / frob_norm
    for sweep_index in range(ITERS):
        product = jnp.einsum('lde,lfe->ldf', polar_iter, polar_iter, precision=highest_prec)
        polar_iter = 1.5 * polar_iter - 0.5 * jnp.einsum('ldf,lfe->lde', product, polar_iter, precision=highest_prec)
    return polar_iter.astype(jnp.bfloat16)

def one_group(group):
    points, targets, centroids, block_list, lengths = group
    list_pick = (block_list[:, None] == jnp.arange(LIST_DEV, dtype=jnp.int32)[None, :]).astype(jnp.float32)
    centre_rows = jnp.dot(list_pick, centroids, precision=highest_prec)
    in_range = jnp.arange(BLK, dtype=jnp.int32)[None, :] < lengths[:, None]
    residual = jnp.where(in_range[:, :, None], points.astype(jnp.float32) - centre_rows[:, None, :], 0.0).astype(jnp.bfloat16)
    block_grams = jnp.einsum('brd,bre->bde', residual.astype(jnp.float32), targets.astype(jnp.float32), precision=highest_prec)
    cross_gram = jnp.einsum('bl,bde->lde', list_pick, block_grams, precision=highest_prec)
    rotation = newton_polar(cross_gram)
    chosen = jnp.einsum('bl,lde->bde', list_pick, rotation.astype(jnp.float32), precision=highest_prec)
    turned = jnp.einsum('brd,bde->bre', residual.astype(jnp.float32), chosen, precision=highest_prec)
    return turned.astype(jnp.bfloat16)

def reference(points, targets, centroids, block_list, lengths, sources):
    groups = NBLK // BLK_DEV
    shaped = (points.reshape(groups, BLK_DEV, BLK, D), targets.reshape(groups, BLK_DEV, BLK, D), centroids.reshape(groups, LIST_DEV, D), block_list.reshape(groups, BLK_DEV), lengths.reshape(groups, BLK_DEV))
    turned = lax.map(one_group, shaped).reshape(NBLK, BLK, D)
    return jnp.take(turned, sources, axis=0)
```

```python
import functools

import jax
import jax.numpy as jnp
from jax import lax
from jax.experimental import pallas as pl
from jax.experimental.pallas import tpu as pltpu
from jax.sharding import PartitionSpec as P

MOVE = 2
ITERS = 5
CORES = 2
VMEM_LIMIT = 48 * 1024 * 1024

f32, bf16, i32 = jnp.float32, jnp.bfloat16, jnp.int32


def assign_slots(bl, ln, first_rows, slot_of_list, plan):
    blocks, lists = bl.shape[0], slot_of_list.shape[0]

    @pl.loop(0, lists)
    def _(l):
        slot_of_list[l] = -1

    def visit(b, nxt, wanted):
        l = bl[b]
        s = slot_of_list[l]
        new = jnp.logical_and(s < 0, wanted)
        slot_of_list[l] = jnp.where(new, nxt, s)
        return nxt + new.astype(i32)

    nxt = jnp.int32(0)
    for b in range(MOVE):
        nxt = visit(b, nxt, True)
    nxt = lax.fori_loop(MOVE, blocks, lambda b, n: visit(b, n, ln[b] > first_rows), nxt, unroll=True)
    plan[blocks] = nxt
    nxt = lax.fori_loop(MOVE, blocks, lambda b, n: visit(b, n, True), nxt, unroll=True)
    for b in range(blocks):
        plan[b] = slot_of_list[bl[b]]


def masked_residual(points, centroid_row, limit):
    rows = lax.broadcasted_iota(i32, points.shape, 0)
    return jnp.where(rows < limit, points.astype(f32) - centroid_row, 0.0).astype(bf16)


def gram_kernel(bl, ln, points, targets, centroids, plan, keep, send, slot_of_list, acc):
    blocks, rows, _ = points.shape
    me = lax.axis_index("narrow")
    core = lax.rem(me, CORES)
    assign_slots(bl, ln, CORES * rows, slot_of_list, plan)
    acc[...] = jnp.zeros_like(acc)

    @pl.loop(0, blocks, unroll=4)
    def _(b):
        slot = plan[b]
        residual = masked_residual(points[b], centroids[pl.ds(bl[b], 1), :], ln[b] - me * rows)
        acc[slot] += lax.dot_general(residual, targets[b], (((0,), (0,)), ((), ())), preferred_element_type=f32)

    @pl.loop(0, keep.shape[0])
    def _(i):
        keep[i] = acc[CORES * i + core]
        send[i] = acc[CORES * i + 1 - core].astype(bf16)


def newton_kernel(count, first, extra, keep, recv, *refs):
    extras, out = refs[:extra], refs[extra]
    xs = []
    for i in range(count):
        g = keep[i] + recv[i].astype(f32)
        for e in extras:
            g = g + e[i].astype(f32)
        xs.append(g * lax.rsqrt(jnp.sum(g * g) + 1e-6))
    for _ in range(ITERS):
        for i in range(count):
            x = xs[i]
            xb = x.astype(bf16)
            p = lax.dot_general(xb, xb, (((1,), (1,)), ((), ())), preferred_element_type=f32).astype(bf16)
            xs[i] = 1.5 * x - 0.5 * jnp.dot(p, xb, preferred_element_type=f32)
    for i in range(count):
        out[i] = xs[i].astype(bf16)


def newton(keep, recv, extras, first, count):
    shape = (count,) + keep.shape[1:]
    flops = count * ITERS * 4 * keep.shape[1] ** 3
    del first
    return pl.pallas_call(
        functools.partial(newton_kernel, count, 0, len(extras)),
        out_shape=jax.ShapeDtypeStruct(shape, bf16),
        in_specs=[pl.BlockSpec(memory_space=pltpu.VMEM)] * (2 + len(extras)),
        out_specs=pl.BlockSpec(memory_space=pltpu.VMEM),
        compiler_params=pltpu.CompilerParams(vmem_limit_bytes=VMEM_LIMIT),
        cost_estimate=pl.CostEstimate(flops=flops, bytes_accessed=count * 10 * 65536, transcendentals=0),
        name="newton",
    )(keep, recv, *extras)


def first_turn_kernel(bl, ln, plan, points, centroids, own, sibling, out):
    _, rows, _ = points.shape
    me = lax.axis_index("narrow")
    core = lax.rem(me, CORES)
    for b in range(MOVE):
        mine = lax.rem(plan[b], CORES) == core
        residual = masked_residual(points[b], centroids[pl.ds(bl[b], 1), :], ln[b] - me * rows)
        rotation = jnp.where(mine, own[0], sibling[0])
        out[b] = jnp.dot(residual, rotation, preferred_element_type=f32).astype(bf16)


def turn_kernel(starts, n_parts, bl, ln, plan, points, centroids, *refs):
    owns, siblings = refs[:n_parts], refs[n_parts:2 * n_parts]
    out, rots = refs[2 * n_parts:]
    blocks, rows, _ = points.shape
    me = lax.axis_index("narrow")
    core = lax.rem(me, CORES)
    for s, o, t in zip(starts, owns, siblings):
        for i in range(o.shape[0]):
            rots[CORES * (s + i) + core] = o[i]
            rots[CORES * (s + i) + 1 - core] = t[i]

    @pl.loop(MOVE, blocks, unroll=6)
    def _(b):
        residual = masked_residual(points[b], centroids[pl.ds(bl[b], 1), :], ln[b] - me * rows)
        out[b] = jnp.dot(residual, rots[plan[b]], preferred_element_type=f32).astype(bf16)


def chunk_sizes(per, capped):
    cap = per * 3 // 4 if capped else per
    sizes, left = [1], cap - 1
    while left > 1:
        sizes.append(min(2, left - 1))
        left -= sizes[-1]
    if left:
        sizes.append(left)
    return sizes, cap


def local(wide, narrow, points, targets, centroids, block_list, lengths, sources):
    blocks, rows, width = points.shape
    lists = centroids.shape[0]
    per = lists // CORES
    chips = narrow // CORES
    smem, vmem = pl.BlockSpec(memory_space=pltpu.SMEM), pl.BlockSpec(memory_space=pltpu.VMEM)
    params = pltpu.CompilerParams(vmem_limit_bytes=VMEM_LIMIT)
    mat = (width, width)

    plan, keep, send = pl.pallas_call(
        gram_kernel,
        out_shape=(
            jax.ShapeDtypeStruct((blocks + 1,), i32),
            jax.ShapeDtypeStruct((per,) + mat, f32),
            jax.ShapeDtypeStruct((per,) + mat, bf16),
        ),
        in_specs=[smem, smem, vmem, vmem, vmem],
        out_specs=(smem, vmem, vmem),
        scratch_shapes=[pltpu.SMEM((lists,), i32), pltpu.VMEM((lists,) + mat, f32)],
        compiler_params=params,
        cost_estimate=pl.CostEstimate(flops=2 * blocks * rows * width * width, bytes_accessed=6 << 20, transcendentals=0),
        name="grams",
    )(block_list, lengths, points, targets, centroids)

    to_core = [(i, i ^ 1) for i in range(narrow)]
    to_chip = [[(i, (i + CORES * k) % narrow) for i in range(narrow)] for k in range(1, chips)]

    sizes, cap = chunk_sizes(per, chips == 2)
    starts = [sum(sizes[:i]) for i in range(len(sizes))]
    bounds = list(zip(starts, sizes))
    all_bounds = bounds + ([(cap, per - cap)] if cap < per else [])

    recvs, chip_sums = [], []
    for s, n in all_bounds:
        recv = lax.ppermute(send[s:s + n], "narrow", to_core)
        recvs.append(recv)
        chip_sums.append((keep[s:s + n] + recv.astype(f32)).astype(bf16))

    def cross(part):
        return tuple(lax.ppermute(part, "narrow", perm) for perm in to_chip)

    crossed = [cross(part) for part in chip_sums[:len(bounds)]]
    if cap < per:
        rest = chip_sums[-1]
        crossed.append(
            lax.cond(plan[blocks] > CORES * cap, cross, lambda part: tuple(jnp.zeros_like(part) for _ in to_chip), rest)
        )

    owns, siblings = [], []
    for (s, n), recv, extras in zip(all_bounds, recvs, crossed):
        own = newton(keep[s:s + n], recv, extras, s, n)
        owns.append(own)
        siblings.append(lax.ppermute(own, "narrow", to_core))

    leading = pl.pallas_call(
        first_turn_kernel,
        out_shape=jax.ShapeDtypeStruct((MOVE, rows, width), bf16),
        in_specs=[smem, smem, smem] + [vmem] * 4,
        out_specs=vmem,
        compiler_params=params,
        cost_estimate=pl.CostEstimate(flops=2 * MOVE * rows * width * width, bytes_accessed=1 << 19, transcendentals=0),
        name="turn_leading",
    )(block_list, lengths, plan, points[:MOVE], centroids, owns[0], siblings[0])

    donors = sources[:MOVE] // blocks
    if wide <= 16 and wide & (wide - 1) == 0:
        here = lax.axis_index("wide")
        parts = [leading] + [lax.ppermute(leading, "wide", [(i, i ^ k) for i in range(wide)]) for k in range(1, wide)]
        hops = jnp.bitwise_xor(donors, here)
    else:
        gathered = lax.all_gather(leading, "wide", axis=0)
        parts = [gathered[k] for k in range(wide)]
        hops = donors
    handed = parts[0]
    for k in range(1, wide):
        handed = jnp.where((hops == k)[:, None, None], parts[k], handed)

    turned = pl.pallas_call(
        functools.partial(turn_kernel, [s for s, _ in all_bounds], len(owns)),
        out_shape=jax.ShapeDtypeStruct((blocks, rows, width), bf16),
        in_specs=[smem, smem, smem] + [vmem] * (2 + 2 * len(owns)),
        out_specs=vmem,
        scratch_shapes=[pltpu.VMEM((lists,) + mat, bf16)],
        compiler_params=params,
        cost_estimate=pl.CostEstimate(flops=2 * blocks * rows * width * width, bytes_accessed=4 << 20, transcendentals=0),
        name="turn",
    )(block_list, lengths, plan, points, centroids, *owns, *siblings)
    return lax.dynamic_update_slice(turned, handed, (0, 0, 0))


def solution(mesh):
    return jax.shard_map(
        functools.partial(local, mesh.shape["wide"], mesh.shape["narrow"]),
        mesh=mesh,
        in_specs=(
            P("wide", "narrow", None),
            P("wide", "narrow", None),
            P("wide", None),
            P("wide"),
            P("wide"),
            P("wide"),
        ),
        out_specs=P("wide", "narrow", None),
        check_vma=False,
    )
```

```python
import functools

import jax
import jax.numpy as jnp
from jax import lax
from jax.experimental import pallas as pl
from jax.experimental.pallas import tpu as pltpu
from jax.sharding import PartitionSpec as P

MOVE = 2
ITERS = 5
CORES = 2
PIECES = 4
VMEM_LIMIT = 14 * 1024 * 1024
LONG = 1 << 30

f32, bf16, i32 = jnp.float32, jnp.bfloat16, jnp.int32

SMEM = pl.BlockSpec(memory_space=pltpu.SMEM)
VMEM = pl.BlockSpec(memory_space=pltpu.VMEM)
HBM = pl.BlockSpec(memory_space=pltpu.HBM)
ANY = pl.BlockSpec(memory_space=pl.ANY)


def stay(x):
    return pltpu.with_memory_space_constraint(x, pltpu.HBM)


def call(kernel, name, outs, in_specs, out_specs, args, moved=1 << 20, scratch=(), aliases={}):
    return pl.pallas_call(
        kernel,
        out_shape=outs,
        in_specs=in_specs,
        out_specs=out_specs,
        scratch_shapes=scratch,
        input_output_aliases=aliases,
        compiler_params=pltpu.CompilerParams(vmem_limit_bytes=VMEM_LIMIT),
        cost_estimate=pl.CostEstimate(flops=16 * moved if moved == LONG else 0, bytes_accessed=moved, transcendentals=0),
        name=name,
    )(*args)


def assign_slots(bl, ln, first_rows, slot_of_list, plan, crossing):
    blocks, lists = bl.shape[0], slot_of_list.shape[0]
    for l in range(lists):
        slot_of_list[l] = -1

    def visit(b, nxt, wanted):
        l = bl[b]
        s = slot_of_list[l]
        new = jnp.logical_and(s < 0, wanted)
        slot_of_list[l] = jnp.where(new, nxt, s)
        return nxt + new.astype(i32)

    nxt = jnp.int32(0)
    for b in range(MOVE):
        nxt = visit(b, nxt, True)
    for b in range(MOVE, blocks):
        nxt = visit(b, nxt, ln[b] > first_rows)
    crossing[0] = nxt
    for b in range(MOVE, blocks):
        nxt = visit(b, nxt, True)
    plan[blocks] = nxt
    for b in range(blocks):
        plan[b] = slot_of_list[bl[b]]


def gram_kernel(bounds, bl_hbm, ln_hbm, points_hbm, targets_hbm, centroids_hbm, plan, crossing, residual, *refs):
    n = len(bounds)
    keeps = refs[:n]
    sends = refs[n:n + 2]
    bl, ln, slot_of_list, points, targets, centroids, acc, sems, int_sems = refs[n + 2:]
    blocks, rows, _ = points.shape
    piece = blocks // PIECES
    copies = [
        pltpu.make_async_copy(bl_hbm, bl, int_sems.at[0]),
        pltpu.make_async_copy(ln_hbm, ln, int_sems.at[1]),
        pltpu.make_async_copy(centroids_hbm, centroids, int_sems.at[2]),
    ]
    for copy in copies:
        copy.start()
    parts = []
    for i in range(PIECES):
        at = pl.ds(i * piece, piece)
        pair = (
            pltpu.make_async_copy(points_hbm.at[at], points.at[at], sems.at[0, i]),
            pltpu.make_async_copy(targets_hbm.at[at], targets.at[at], sems.at[1, i]),
        )
        for copy in pair:
            copy.start()
        parts.append(pair)
    me = lax.axis_index("narrow")
    core = lax.rem(me, CORES)
    copies[0].wait()
    copies[1].wait()
    assign_slots(bl, ln, CORES * rows, slot_of_list, plan, crossing)
    acc[...] = jnp.zeros_like(acc)
    copies[2].wait()
    row_ids = lax.broadcasted_iota(i32, points.shape[1:], 0) + me * rows
    for i in range(PIECES):
        for copy in parts[i]:
            copy.wait()

        @pl.loop(i * piece, (i + 1) * piece, unroll=4)
        def _(b):
            slot = plan[b]
            kept = row_ids < ln[b]
            res = jnp.where(kept, points[b].astype(f32) - centroids[pl.ds(bl[b], 1), :], 0.0).astype(bf16)
            residual[b] = res
            acc[slot] += lax.dot_general(res, targets[b], (((0,), (0,)), ((), ())), preferred_element_type=f32)

    for (s, count), keep in zip(bounds, keeps):
        for i in range(count):
            at = CORES * (s + i)
            keep[i] = acc[at + core]
            send, j = (sends[0], i) if s == 0 else (sends[1], s + i - bounds[0][1])
            send[j] = acc[at + 1 - core].astype(bf16)


def sum_kernel(bounds, base, *refs):
    n = len(bounds)
    keeps, recv, sums = refs[:n], refs[n], refs[-n:]
    for (s, count), keep, out in zip(bounds, keeps, sums):
        at = s - base
        out[...] = (keep[...] + recv[at:at + count].astype(f32)).astype(bf16)


def newton_kernel(count, extra, first, offset, keep, recv, *refs):
    extras, out = refs[:extra], refs[-1]

    def run():
        xs = []
        for i in range(count):
            g = keep[i] + recv[offset + i].astype(f32)
            for e in extras:
                g = g + e[i].astype(f32)
            xs.append(g * lax.rsqrt(jnp.sum(g * g) + 1e-6))
        for _ in range(ITERS):
            for i in range(count):
                x = xs[i]
                xb = x.astype(bf16)
                p = lax.dot_general(xb, xb, (((1,), (1,)), ((), ())), preferred_element_type=f32).astype(bf16)
                xs[i] = 1.5 * x - 0.5 * jnp.dot(p, xb, preferred_element_type=f32)
        for i in range(count):
            out[i] = xs[i].astype(bf16)

    if first is None:
        run()
    else:
        plan = refs[-2]
        used = plan[plan.shape[0] - 1] > CORES * first
        pl.when(used)(run)

        @pl.when(jnp.logical_not(used))
        def _():
            out[...] = jnp.zeros_like(out)


def newton(keep, recv, extras, after, first, offset, plan=None, moved=1 << 20):
    count, width = keep.shape[:2]
    args = (keep, recv) + tuple(extras) + tuple(after)
    specs = [VMEM] * (2 + len(extras)) + [ANY] * len(after)
    if plan is not None:
        args, specs = args + (plan,), specs + [SMEM]
    return call(
        functools.partial(newton_kernel, count, len(extras), first if plan is not None else None, offset),
        "newton",
        jax.ShapeDtypeStruct(keep.shape, bf16),
        specs,
        VMEM,
        args,
        moved=moved,
    )


def leading_kernel(plan, residual, own, sibling, out):
    core = lax.rem(lax.axis_index("narrow"), CORES)
    for b in range(MOVE):
        mine = lax.rem(plan[b], CORES) == core
        rotation = jnp.where(mine, own[0], sibling[0])
        out[b] = jnp.dot(residual[b], rotation, preferred_element_type=f32).astype(bf16)


def pair_kernel(near, far, _, out):
    out[0] = near[...]
    out[1] = far[...]


def turn_kernel(starts, hops, plan, sources, residual, *refs):
    n = len(starts)
    owns, siblings = refs[:n], refs[n:2 * n]
    parts = refs[2 * n:2 * n + len(hops)]
    out, rots, turned, sems = refs[2 * n + len(hops):]
    blocks, rows, _ = residual.shape
    piece = blocks // PIECES
    core = lax.rem(lax.axis_index("narrow"), CORES)
    here = lax.axis_index("wide")
    for s, o, t in zip(starts, owns, siblings):
        for i in range(o.shape[0]):
            rots[CORES * (s + i) + core] = o[i]
            rots[CORES * (s + i) + 1 - core] = t[i]
    for j in range(MOVE):
        donor = sources[j] // blocks
        picked = parts[0][0, j]
        for part, group in zip(parts, hops):
            for i, hop in enumerate(group):
                match = donor == (hop if len(parts) == 1 else here ^ hop)
                picked = jnp.where(match, part[i, j], picked)
        turned[j] = picked
    copies = []
    for i in range(PIECES):
        @pl.loop(max(MOVE, i * piece), (i + 1) * piece, unroll=True)
        def _(b):
            turned[b] = jnp.dot(residual[b], rots[plan[b]], preferred_element_type=f32).astype(bf16)

        at = pl.ds(i * piece, piece)
        copies.append(pltpu.make_async_copy(turned.at[at], out.at[at], sems.at[i]))
        copies[-1].start()
    for copy in copies:
        copy.wait()


def turn_rest_kernel(first, plan, residual, own, sibling, _, out, block):
    core = lax.rem(lax.axis_index("narrow"), CORES)

    @pl.loop(MOVE, residual.shape[0])
    def _(b):
        @pl.when(plan[b] >= first)
        def _():
            at = lax.div(plan[b] - first, CORES)
            mine = lax.rem(plan[b], CORES) == core
            rotation = jnp.where(mine, own[at], sibling[at])
            block[...] = jnp.dot(residual[b], rotation, preferred_element_type=f32).astype(bf16)
            pltpu.sync_copy(block, out.at[b])


def chunk_bounds(per, capped):
    cap = per * 3 // 4 if capped else per
    sizes, left = [1], cap - 1
    while left > 1:
        sizes.append(min(2, left - 1))
        left -= sizes[-1]
    if left:
        sizes.append(left)
    bounds = [(sum(sizes[:i]), size) for i, size in enumerate(sizes)]
    return bounds, [(cap, per - cap)] if cap < per else []


def local(wide, narrow, points, targets, centroids, block_list, lengths, sources):
    blocks, rows, width = points.shape
    lists = centroids.shape[0]
    per = lists // CORES
    chips = narrow // CORES
    mat = (width, width)
    bounds, rest = chunk_bounds(per, chips == 2)
    all_bounds = bounds + rest

    n = len(all_bounds)
    lead = all_bounds[0][1]
    grams = call(
        functools.partial(gram_kernel, all_bounds),
        "grams",
        (jax.ShapeDtypeStruct((blocks + 1,), i32), jax.ShapeDtypeStruct((1,), i32), jax.ShapeDtypeStruct(points.shape, bf16))
        + tuple(jax.ShapeDtypeStruct((count,) + mat, f32) for _, count in all_bounds)
        + tuple(jax.ShapeDtypeStruct((count,) + mat, bf16) for count in (lead, per - lead)),
        [HBM] * 5,
        (SMEM, SMEM) + (VMEM,) * (3 + n),
        tuple(stay(x) for x in (block_list, lengths, points, targets, centroids)),
        scratch=[
            pltpu.SMEM((blocks,), i32),
            pltpu.SMEM((blocks,), i32),
            pltpu.SMEM((lists,), i32),
            pltpu.VMEM(points.shape, bf16),
            pltpu.VMEM(points.shape, bf16),
            pltpu.VMEM(centroids.shape, f32),
            pltpu.VMEM((lists,) + mat, f32),
            pltpu.SemaphoreType.DMA((2, PIECES)),
            pltpu.SemaphoreType.DMA((3,)),
        ],
    )
    plan, crossing, residual = grams[:3]
    keeps, sends = grams[3:3 + n], grams[3 + n:]

    to_core = [(i, i ^ 1) for i in range(narrow)]
    to_chip = [[(i, (i + CORES * k) % narrow) for i in range(narrow)] for k in range(1, chips)]

    def cross(part):
        return tuple(lax.ppermute(part, "narrow", perm) for perm in to_chip)

    def sums_of(some, recv, base, after=(), keeps=keeps):
        return call(
            functools.partial(sum_kernel, all_bounds[some], base),
            "chip_sums",
            tuple(jax.ShapeDtypeStruct((count,) + mat, bf16) for _, count in all_bounds[some]),
            [VMEM] * (1 + len(all_bounds[some])) + [ANY] * len(after),
            (VMEM,) * len(all_bounds[some]),
            (*(keeps[some] if len(keeps) == n else keeps), recv, *after),
        )

    recvs = [lax.ppermute(send, "narrow", to_core) for send in sends]
    sums = sums_of(slice(0, 1), recvs[0], 0)
    m = len(bounds)
    sums += sums_of(slice(1, m), recvs[1], lead, sums)
    crossed = [cross(part) for part in sums[:len(bounds)]]
    crossed += [()] * len(rest)

    owns, siblings = [None] * n, [None] * n

    def polar(i, after=(), gate=None):
        s = all_bounds[i][0]
        recv, offset = (recvs[0], 0) if i == 0 else (recvs[1], s - lead)
        owns[i] = newton(keeps[i], recv, crossed[i], after, s, offset, gate, LONG if 2 <= i < len(bounds) else 1 << 20)
        siblings[i] = lax.ppermute(owns[i], "narrow", to_core)

    if rest:
        polar(n - 1, sums, plan)
    polar(0, (owns[-1],) if rest else ())

    leading = call(
        leading_kernel,
        "turn_leading",
        jax.ShapeDtypeStruct((MOVE, rows, width), bf16),
        [SMEM] + [VMEM] * 3,
        VMEM,
        (plan, residual, owns[0], siblings[0]),
    )
    if wide <= 16 and wide & (wide - 1) == 0:
        half = wide // 2
        far = lax.ppermute(leading, "wide", [(i, i ^ half) for i in range(wide)])
        polar(1, (leading,))
        pair = call(
            pair_kernel,
            "pair",
            jax.ShapeDtypeStruct((2,) + leading.shape, bf16),
            [VMEM, VMEM, ANY],
            VMEM,
            (leading, far, owns[1]),
        )
        parts = [pair] + [lax.ppermute(pair, "wide", [(i, i ^ k) for i in range(wide)]) for k in range(1, half)]
        hops = [(k, k ^ half) for k in range(half)]
    else:
        polar(1, (leading,))
        parts = [lax.all_gather(leading, "wide", axis=0)]
        hops = [tuple(range(wide))]

    for i in range(2, len(bounds)):
        polar(i, (owns[i - 1],) if i > 2 else (owns[1], parts[0]))

    turned = call(
        functools.partial(turn_kernel, [s for s, _ in all_bounds], hops),
        "turn",
        pltpu.HBM(points.shape, bf16),
        [SMEM] * 2 + [VMEM] * (1 + 2 * n + len(parts)),
        HBM,
        (plan, sources, residual, *owns, *siblings, *parts),
        scratch=[
            pltpu.VMEM((lists,) + mat, bf16),
            pltpu.VMEM(points.shape, bf16),
            pltpu.SemaphoreType.DMA((PIECES,)),
        ],
    )
    if not rest:
        return turned

    def exchange_rest(_, state):
        turned, keep = state
        chip = sums_of(slice(m, n), recvs[1], lead, keeps=(keep,))[0]
        own = newton(keep, recvs[1], cross(chip), (), None, rest[0][0] - lead)
        sibling = lax.ppermute(own, "narrow", to_core)
        turned = call(
            functools.partial(turn_rest_kernel, CORES * rest[0][0]),
            "turn_rest",
            pltpu.HBM(turned.shape, bf16),
            [SMEM] + [VMEM] * 3 + [HBM],
            HBM,
            (plan, residual, own, sibling, stay(turned)),
            scratch=[pltpu.VMEM((rows, width), bf16)],
            aliases={4: 0},
        )
        return turned, own.astype(f32)

    overflow = (crossing[0] > CORES * rest[0][0]).astype(i32)
    return lax.fori_loop(0, overflow, exchange_rest, (turned, keeps[-1]))[0]


def solution(mesh):
    return jax.shard_map(
        functools.partial(local, mesh.shape["wide"], mesh.shape["narrow"]),
        mesh=mesh,
        in_specs=(
            P("wide", "narrow", None),
            P("wide", "narrow", None),
            P("wide", None),
            P("wide"),
            P("wide"),
            P("wide"),
        ),
        out_specs=P("wide", "narrow", None),
        check_vma=False,
    )
```

```python
import functools

import jax
import jax.numpy as jnp
from jax import lax
from jax.experimental import pallas as pl
from jax.experimental.pallas import tpu as pltpu
from jax.sharding import PartitionSpec as P

MOVE = 2
ITERS = 5
CORES = 2
PIECES = 2
VMEM_LIMIT = 14 * 1024 * 1024
LONG = 1 << 30

f32, bf16, i32 = jnp.float32, jnp.bfloat16, jnp.int32

SMEM = pl.BlockSpec(memory_space=pltpu.SMEM)
VMEM = pl.BlockSpec(memory_space=pltpu.VMEM)
HBM = pl.BlockSpec(memory_space=pltpu.HBM)
ANY = pl.BlockSpec(memory_space=pl.ANY)


def stay(x):
    return pltpu.with_memory_space_constraint(x, pltpu.HBM)


def call(kernel, name, outs, in_specs, out_specs, args, moved=1 << 20, scratch=(), aliases={}):
    return pl.pallas_call(
        kernel,
        out_shape=outs,
        in_specs=in_specs,
        out_specs=out_specs,
        scratch_shapes=scratch,
        input_output_aliases=aliases,
        compiler_params=pltpu.CompilerParams(vmem_limit_bytes=VMEM_LIMIT),
        cost_estimate=pl.CostEstimate(flops=16 * moved if moved == LONG else 0, bytes_accessed=moved, transcendentals=0),
        name=name,
    )(*args)


def assign_slots(bl, ln, first_rows, slot_of_list, plan, crossing):
    blocks, lists = bl.shape[0], slot_of_list.shape[0]
    for l in range(lists):
        slot_of_list[l] = -1

    def visit(b, nxt, wanted):
        l = bl[b]
        s = slot_of_list[l]
        new = jnp.logical_and(s < 0, wanted)
        slot_of_list[l] = jnp.where(new, nxt, s)
        return nxt + new.astype(i32)

    nxt = jnp.int32(0)
    for b in range(MOVE):
        nxt = visit(b, nxt, True)
    for b in range(MOVE, blocks):
        nxt = visit(b, nxt, ln[b] > first_rows)
    crossing[0] = nxt
    for b in range(MOVE, blocks):
        nxt = visit(b, nxt, True)
    plan[blocks] = nxt
    for b in range(blocks):
        plan[b] = slot_of_list[bl[b]]


def gram_kernel(bl_hbm, ln_hbm, points_hbm, targets_hbm, centroids_hbm, plan, crossing, residual, acc, send, *scratch):
    bl, ln, slot_of_list, points, targets, centroids, sems, int_sems = scratch
    blocks, rows, _ = points.shape
    per = acc.shape[0] // CORES
    piece = blocks // PIECES
    copies = [
        pltpu.make_async_copy(bl_hbm, bl, int_sems.at[0]),
        pltpu.make_async_copy(ln_hbm, ln, int_sems.at[1]),
        pltpu.make_async_copy(centroids_hbm, centroids, int_sems.at[2]),
    ]
    for copy in copies:
        copy.start()
    parts = []
    for i in range(PIECES):
        at = pl.ds(i * piece, piece)
        pair = (
            pltpu.make_async_copy(points_hbm.at[at], points.at[at], sems.at[0, i]),
            pltpu.make_async_copy(targets_hbm.at[at], targets.at[at], sems.at[1, i]),
        )
        for copy in pair:
            copy.start()
        parts.append(pair)
    me = lax.axis_index("narrow")
    core = lax.rem(me, CORES)
    acc[...] = jnp.zeros_like(acc)
    copies[0].wait()
    copies[1].wait()
    assign_slots(bl, ln, CORES * rows, slot_of_list, plan, crossing)
    copies[2].wait()
    row_ids = lax.broadcasted_iota(i32, points.shape[1:], 0) + me * rows
    for i in range(PIECES):
        for copy in parts[i]:
            copy.wait()
        for b in range(i * piece, (i + 1) * piece):
            kept = row_ids < ln[b]
            res = jnp.where(kept, points[b].astype(f32) - centroids[pl.ds(bl[b], 1), :], 0.0).astype(bf16)
            residual[b] = res
            slot = plan[b]
            at = lax.div(slot, CORES) + jnp.where(lax.rem(slot, CORES) == core, 0, per)
            acc[at] += lax.dot_general(res, targets[b], (((0,), (0,)), ((), ())), preferred_element_type=f32)
    for i in range(send.shape[0]):
        send[i] = acc[per + i].astype(bf16)


def lead_sum_kernel(per, acc, recv, chip, send):
    lead = recv.shape[0]
    chip[...] = (acc[:lead] + recv[...].astype(f32)).astype(bf16)
    for i in range(send.shape[0]):
        send[i] = acc[per + lead + i].astype(bf16)


def sum_kernel(first, acc, recv, *sums):
    at = 0
    for out in sums:
        count = out.shape[0]
        out[...] = (acc[first + at:first + at + count] + recv[at:at + count].astype(f32)).astype(bf16)
        at += count


def newton_kernel(count, first, offset, extra, gated, acc, recv, *refs):
    pieces, out, chip = refs[:-2], refs[-2], refs[-1]

    def run():
        xs = []
        for i in range(count):
            g = acc[first + i] + recv[offset + i].astype(f32)
            if gated:
                chip[i] = g
            for which in extra:
                piece, row = which[i]
                g = g + pieces[piece][row].astype(f32)
            xs.append(g)
        polar(xs, out)

    if not gated:
        run()
    else:
        plan = refs[-3]
        used = plan[plan.shape[0] - 1] > CORES * first
        pl.when(used)(run)

        @pl.when(jnp.logical_not(used))
        def _():
            out[...] = jnp.zeros_like(out)
            chip[...] = jnp.zeros_like(chip)


def polar(grams, out):
    xs = []
    for g in grams:
        gb = g.astype(bf16)
        p = lax.dot_general(gb, gb, (((1,), (1,)), ((), ())), preferred_element_type=f32)
        scale = lax.rsqrt(jnp.sum(g * g) + 1e-6)
        p = (p * (scale * scale)).astype(bf16)
        xs.append((1.5 * scale) * g - (0.5 * scale) * jnp.dot(p, gb, preferred_element_type=f32))
    for _ in range(ITERS - 1):
        for i, x in enumerate(xs):
            xb = x.astype(bf16)
            p = lax.dot_general(xb, xb, (((1,), (1,)), ((), ())), preferred_element_type=f32).astype(bf16)
            xs[i] = 1.5 * x - 0.5 * jnp.dot(p, xb, preferred_element_type=f32)
    for i, x in enumerate(xs):
        out[i] = x.astype(bf16)


def newton(acc, first, count, recv, offset, crossed, after=(), plan=None, moved=1 << 20):
    extra = [[] for _ in (crossed[0] if crossed else ())]
    flat = []
    for group in crossed:
        for chip, part in enumerate(group):
            extra[chip] += [(len(flat), row) for row in range(part.shape[0])]
            flat.append(part)
    gated = plan is not None
    args = (acc, recv, *flat, *after) + ((plan,) if gated else ())
    specs = [VMEM] * (2 + len(flat)) + [ANY] * len(after) + [SMEM] * gated
    shape = (count,) + acc.shape[1:]
    out = call(
        functools.partial(newton_kernel, count, first, offset, extra, gated),
        "newton",
        (jax.ShapeDtypeStruct(shape, bf16),) + ((jax.ShapeDtypeStruct(shape, f32),) if gated else ()),
        specs,
        (VMEM,) * (1 + gated),
        args,
        moved=moved,
        scratch=[] if gated else [pltpu.VMEM((8, 128), f32)],
    )
    return out if gated else out[0]


def newton_rest_kernel(others, chip, *refs):
    out = refs[-1]
    grams = []
    for i in range(chip.shape[0]):
        g = chip[i]
        for other in refs[:others]:
            g = g + other[i].astype(f32)
        grams.append(g)
    polar(grams, out)


def leading_kernel(plan, residual, own, sibling, out):
    core = lax.rem(lax.axis_index("narrow"), CORES)
    for b in range(MOVE):
        mine = lax.rem(plan[b], CORES) == core
        rotation = jnp.where(mine, own[0], sibling[0])
        out[b] = jnp.dot(residual[b], rotation, preferred_element_type=f32).astype(bf16)


def pair_kernel(near, far, out):
    out[0] = near[...]
    out[1] = far[...]


def place_kernel(hops, blocks, sources, *refs):
    parts, out = refs[:len(hops)], refs[-1]
    here = lax.axis_index("wide")
    for j in range(MOVE):
        donor = lax.div(sources[j], blocks)
        picked = parts[0][0, j]
        for part, group in zip(parts, hops):
            for i, hop in enumerate(group):
                match = donor == (hop if len(parts) == 1 else here ^ hop)
                picked = jnp.where(match, part[i, j], picked)
        out[j] = picked


def turn_kernel(starts, plan, handed, residual, *refs):
    n = len(starts)
    owns, siblings = refs[:n], refs[n:2 * n]
    out, rots, turned, sems = refs[2 * n:]
    blocks, rows, _ = residual.shape
    piece = blocks // PIECES
    core = lax.rem(lax.axis_index("narrow"), CORES)
    for s, o, t in zip(starts, owns, siblings):
        for i in range(o.shape[0]):
            rots[CORES * (s + i) + core] = o[i]
            rots[CORES * (s + i) + 1 - core] = t[i]
    copies = []
    for i in range(PIECES):
        for b in range(i * piece, (i + 1) * piece):
            if b < MOVE:
                turned[b] = handed[b]
            else:
                turned[b] = jnp.dot(residual[b], rots[plan[b]], preferred_element_type=f32).astype(bf16)
        at = pl.ds(i * piece, piece)
        copies.append(pltpu.make_async_copy(turned.at[at], out.at[at], sems.at[i]))
        copies[-1].start()
    for copy in copies:
        copy.wait()


def turn_rest_kernel(first, bl, ln, plan, own, sibling, centroids, points_hbm, _, out, block):
    blocks, rows, _ = points_hbm.shape
    me = lax.axis_index("narrow")
    core = lax.rem(me, CORES)
    row_ids = lax.broadcasted_iota(i32, block.shape, 0) + me * rows

    @pl.loop(MOVE, blocks)
    def _(b):
        @pl.when(plan[b] >= first)
        def _():
            pltpu.sync_copy(points_hbm.at[b], block)
            kept = row_ids < ln[b]
            residual = jnp.where(kept, block[...].astype(f32) - centroids[pl.ds(bl[b], 1), :], 0.0).astype(bf16)
            at = lax.div(plan[b] - first, CORES)
            mine = lax.rem(plan[b], CORES) == core
            rotation = jnp.where(mine, own[at], sibling[at])
            block[...] = jnp.dot(residual, rotation, preferred_element_type=f32).astype(bf16)
            pltpu.sync_copy(block, out.at[b])


def pieces_of(count):
    return [count - count // 2, count // 2] if count > 1 else [count]


def local(wide, narrow, points, targets, centroids, block_list, lengths, sources):
    blocks, rows, width = points.shape
    lists = centroids.shape[0]
    per = lists // CORES
    chips = narrow // CORES
    mat = (width, width)
    lead = MOVE // CORES
    cap = per * 3 // 4 if chips == 2 else per
    rest = per - cap

    plan, crossing, residual, acc, send = call(
        gram_kernel,
        "grams",
        (
            jax.ShapeDtypeStruct((blocks + 1,), i32),
            jax.ShapeDtypeStruct((1,), i32),
            jax.ShapeDtypeStruct(points.shape, bf16),
            jax.ShapeDtypeStruct((lists,) + mat, f32),
            jax.ShapeDtypeStruct((lead,) + mat, bf16),
        ),
        [HBM] * 5,
        (SMEM, SMEM, VMEM, VMEM, VMEM),
        tuple(stay(x) for x in (block_list, lengths, points, targets, centroids)),
        scratch=[
            pltpu.SMEM((blocks,), i32),
            pltpu.SMEM((blocks,), i32),
            pltpu.SMEM((lists,), i32),
            pltpu.VMEM(points.shape, bf16),
            pltpu.VMEM(points.shape, bf16),
            pltpu.VMEM(centroids.shape, f32),
            pltpu.SemaphoreType.DMA((2, PIECES)),
            pltpu.SemaphoreType.DMA((3,)),
        ],
    )

    to_core = [(i, i ^ 1) for i in range(narrow)]
    to_chip = [[(i, (i + CORES * k) % narrow) for i in range(narrow)] for k in range(1, chips)]

    def cross(part):
        return tuple(lax.ppermute(part, "narrow", perm) for perm in to_chip)

    def swap(part):
        return lax.ppermute(part, "narrow", to_core)

    recv = swap(send)
    lead_chip, send_others = call(
        functools.partial(lead_sum_kernel, per),
        "lead_sum",
        (jax.ShapeDtypeStruct((lead,) + mat, bf16), jax.ShapeDtypeStruct((per - lead,) + mat, bf16)),
        [VMEM, VMEM],
        (VMEM, VMEM),
        (acc, recv),
    )
    lead_crossed = cross(lead_chip)
    recv_others = swap(send_others)

    def chip_sums(counts):
        return call(
            functools.partial(sum_kernel, lead),
            "chip_sums",
            tuple(jax.ShapeDtypeStruct((count,) + mat, bf16) for count in counts),
            [VMEM, VMEM],
            (VMEM,) * len(counts),
            (acc, recv_others),
        )

    main_chips = chip_sums(pieces_of(cap - lead))
    main_crossed = [cross(part) for part in main_chips]
    tokens = main_chips
    starts, owns = [0, lead], [None, None]
    if rest:
        starts.append(cap)
        own, rest_chip = newton(acc, cap, rest, recv_others, cap - lead, (), tokens, plan, 1 << 12)
        owns.append(own)
        tokens = (own,)
    owns[0] = newton(acc, 0, lead, recv, 0, (lead_crossed,), tokens)
    siblings = [swap(owns[0])] + [None] * (len(owns) - 1)

    leading = call(
        leading_kernel,
        "turn_leading",
        jax.ShapeDtypeStruct((MOVE, rows, width), bf16),
        [SMEM] + [VMEM] * 3,
        VMEM,
        (plan, residual, owns[0], siblings[0]),
    )
    if wide <= 16 and wide & (wide - 1) == 0:
        half = wide // 2
        far = lax.ppermute(leading, "wide", [(i, i ^ half) for i in range(wide)])
        pair = call(
            pair_kernel,
            "pair",
            jax.ShapeDtypeStruct((2,) + leading.shape, bf16),
            [VMEM, VMEM],
            VMEM,
            (leading, far),
        )
        parts = [pair] + [lax.ppermute(pair, "wide", [(i, i ^ k) for i in range(wide)]) for k in range(1, half)]
        hops = [(k, k ^ half) for k in range(half)]
        token = pair
    else:
        parts = [lax.all_gather(leading, "wide", axis=0)]
        hops = [tuple(range(wide))]
        token = leading

    owns[1] = newton(acc, lead, cap - lead, recv_others, 0, main_crossed, (token,))
    siblings[1:] = [swap(own) for own in owns[1:]]

    handed = call(
        functools.partial(place_kernel, hops, blocks),
        "place",
        jax.ShapeDtypeStruct(leading.shape, bf16),
        [SMEM] + [VMEM] * len(parts) + [ANY],
        VMEM,
        (sources, *parts, owns[1]),
        moved=LONG,
    )
    turned = call(
        functools.partial(turn_kernel, starts),
        "turn",
        pltpu.HBM(points.shape, bf16),
        [SMEM] + [VMEM] * (2 + 2 * len(owns)),
        HBM,
        (plan, handed, residual, *owns, *siblings),
        scratch=[
            pltpu.VMEM((lists,) + mat, bf16),
            pltpu.VMEM(points.shape, bf16),
            pltpu.SemaphoreType.DMA((PIECES,)),
        ],
    )
    if not rest:
        return turned

    def exchange_rest(state):
        crossing, turned, chip = state
        own = call(
            functools.partial(newton_rest_kernel, len(to_chip)),
            "newton_rest",
            jax.ShapeDtypeStruct(chip.shape, bf16),
            [VMEM] * (1 + len(to_chip)),
            VMEM,
            (chip, *cross(chip.astype(bf16))),
        )
        turned = call(
            functools.partial(turn_rest_kernel, CORES * cap),
            "turn_rest",
            pltpu.HBM(turned.shape, bf16),
            [SMEM] * 3 + [VMEM] * 3 + [HBM] * 2,
            HBM,
            (block_list, lengths, plan, own, swap(own), centroids, stay(points), stay(turned)),
            scratch=[pltpu.VMEM((rows, width), bf16)],
            aliases={7: 0},
        )
        return jnp.zeros_like(crossing), turned, own.astype(f32)

    state = (crossing, turned, rest_chip)
    return lax.while_loop(lambda state: state[0][0] > CORES * cap, exchange_rest, state)[1]


def solution(mesh):
    return jax.shard_map(
        functools.partial(local, mesh.shape["wide"], mesh.shape["narrow"]),
        mesh=mesh,
        in_specs=(
            P("wide", "narrow", None),
            P("wide", "narrow", None),
            P("wide", None),
            P("wide"),
            P("wide"),
            P("wide"),
        ),
        out_specs=P("wide", "narrow", None),
        check_vma=False,
    )
```

```python
import functools

import jax
import jax.numpy as jnp
from jax import lax
from jax.experimental import pallas as pl
from jax.experimental.pallas import tpu as pltpu
from jax.sharding import PartitionSpec as P

MOVE = 2
ITERS = 5
CORES = 2
PIECES = 2
VMEM_LIMIT = 14 * 1024 * 1024
LONG = 1 << 30
GROUP = 4
LEAD_FLOPS = 2800000000
PAIR_FLOPS = 0

f32, bf16, i32 = jnp.float32, jnp.bfloat16, jnp.int32

SMEM = pl.BlockSpec(memory_space=pltpu.SMEM)
VMEM = pl.BlockSpec(memory_space=pltpu.VMEM)
HBM = pl.BlockSpec(memory_space=pltpu.HBM)
ANY = pl.BlockSpec(memory_space=pl.ANY)


def stay(x):
    return pltpu.with_memory_space_constraint(x, pltpu.HBM)


def call(kernel, name, outs, in_specs, out_specs, args, moved=1 << 20, flops=0, scratch=(), aliases={}):
    return pl.pallas_call(
        kernel,
        out_shape=outs,
        in_specs=in_specs,
        out_specs=out_specs,
        scratch_shapes=scratch,
        input_output_aliases=aliases,
        compiler_params=pltpu.CompilerParams(vmem_limit_bytes=VMEM_LIMIT),
        cost_estimate=pl.CostEstimate(flops=16 * moved if moved == LONG else flops, bytes_accessed=moved, transcendentals=0),
        name=name,
    )(*args)


def assign_slots(bl, ln, first_rows, slot_of_list, plan, crossing):
    blocks, lists = bl.shape[0], slot_of_list.shape[0]
    for l in range(lists):
        slot_of_list[l] = -1

    def visit(b, nxt, wanted):
        l = bl[b]
        s = slot_of_list[l]
        new = jnp.logical_and(s < 0, wanted)
        slot_of_list[l] = jnp.where(new, nxt, s)
        return nxt + new.astype(i32)

    nxt = jnp.int32(0)
    for b in range(MOVE):
        nxt = visit(b, nxt, True)
    for b in range(MOVE, blocks):
        nxt = visit(b, nxt, ln[b] > first_rows)
    crossing[0] = nxt
    for b in range(MOVE, blocks):
        nxt = visit(b, nxt, True)
    plan[blocks] = nxt
    for b in range(blocks):
        plan[b] = slot_of_list[bl[b]]


def gram_kernel(bl_hbm, ln_hbm, sources_hbm, points_hbm, targets_hbm, centroids_hbm, plan, crossing, residual, same, acc, send, *scratch):
    bl, ln, sources, slot_of_list, points, targets, centroids, sems, int_sems = scratch
    blocks, rows, _ = points.shape
    per = acc.shape[0] // CORES
    piece = blocks // PIECES
    copies = [
        pltpu.make_async_copy(bl_hbm, bl, int_sems.at[0]),
        pltpu.make_async_copy(ln_hbm, ln, int_sems.at[1]),
        pltpu.make_async_copy(centroids_hbm, centroids, int_sems.at[2]),
        pltpu.make_async_copy(sources_hbm, sources, int_sems.at[3]),
    ]
    for copy in copies:
        copy.start()
    parts = []
    for i in range(PIECES):
        at = pl.ds(i * piece, piece)
        pair = (
            pltpu.make_async_copy(points_hbm.at[at], points.at[at], sems.at[0, i]),
            pltpu.make_async_copy(targets_hbm.at[at], targets.at[at], sems.at[1, i]),
        )
        for copy in pair:
            copy.start()
        parts.append(pair)
    me = lax.axis_index("narrow")
    core = lax.rem(me, CORES)
    acc[...] = jnp.zeros_like(acc)
    copies[0].wait()
    copies[1].wait()
    assign_slots(bl, ln, CORES * rows, slot_of_list, plan, crossing)
    copies[2].wait()
    copies[3].wait()
    for j in range(MOVE):
        plan[blocks + 1 + j] = lax.div(sources[j], blocks)
        mine = lax.rem(plan[j], CORES) == core
        same[j] = jnp.full(same.shape[1:], jnp.where(mine, 1.0, 0.0), f32)
    row_ids = lax.broadcasted_iota(i32, points.shape[1:], 0) + me * rows
    for i in range(PIECES):
        for copy in parts[i]:
            copy.wait()
        for b in range(i * piece, (i + 1) * piece):
            kept = row_ids < ln[b]
            res = jnp.where(kept, points[b].astype(f32) - centroids[pl.ds(bl[b], 1), :], 0.0).astype(bf16)
            residual[b] = res
            slot = plan[b]
            at = lax.div(slot, CORES) + jnp.where(lax.rem(slot, CORES) == core, 0, per)
            acc[at] += lax.dot_general(res, targets[b], (((0,), (0,)), ((), ())), preferred_element_type=f32)
    for i in range(send.shape[0]):
        send[i] = acc[per + i].astype(bf16)


def lead_sum_kernel(per, acc, recv, chip, send):
    lead = recv.shape[0]
    chip[...] = (acc[:lead] + recv[...].astype(f32)).astype(bf16)
    for i in range(send.shape[0]):
        send[i] = acc[per + lead + i].astype(bf16)


def sum_kernel(first, acc, recv, *sums):
    at = 0
    for out in sums:
        count = out.shape[0]
        out[...] = (acc[first + at:first + at + count] + recv[at:at + count].astype(f32)).astype(bf16)
        at += count


def newton_kernel(count, first, offset, extra, gated, acc, recv, *refs):
    pieces, out, chip = refs[:-2], refs[-2], refs[-1]

    def run():
        xs = []
        for i in range(count):
            g = acc[first + i] + recv[offset + i].astype(f32)
            if gated:
                chip[i] = g
            for which in extra:
                piece, row = which[i]
                g = g + pieces[piece][row].astype(f32)
            xs.append(g)
        polar(xs, out)

    if not gated:
        run()
    else:
        plan = refs[-3]
        used = plan[plan.shape[0] - 1 - MOVE] > CORES * first
        pl.when(used)(run)

        @pl.when(jnp.logical_not(used))
        def _():
            out[...] = jnp.zeros_like(out)
            chip[...] = jnp.zeros_like(chip)


def polar(grams, out):
    xs = []
    for g in grams:
        gb = g.astype(bf16)
        p = lax.dot_general(gb, gb, (((1,), (1,)), ((), ())), preferred_element_type=f32)
        scale = lax.rsqrt(jnp.sum(g * g) + 1e-6)
        p = (p * (scale * scale)).astype(bf16)
        xs.append((1.5 * scale) * g - (0.5 * scale) * jnp.dot(p, gb, preferred_element_type=f32))
    for _ in range(ITERS - 1):
        for i, x in enumerate(xs):
            xb = x.astype(bf16)
            p = lax.dot_general(xb, xb, (((1,), (1,)), ((), ())), preferred_element_type=f32).astype(bf16)
            xs[i] = 1.5 * x - 0.5 * jnp.dot(p, xb, preferred_element_type=f32)
    for i, x in enumerate(xs):
        out[i] = x.astype(bf16)


def newton(acc, first, count, recv, offset, crossed, after=(), plan=None, moved=1 << 20):
    extra = [[] for _ in (crossed[0] if crossed else ())]
    flat = []
    for group in crossed:
        for chip, part in enumerate(group):
            extra[chip] += [(len(flat), row) for row in range(part.shape[0])]
            flat.append(part)
    gated = plan is not None
    args = (acc, recv, *flat, *after) + ((plan,) if gated else ())
    specs = [VMEM] * (2 + len(flat)) + [ANY] * len(after) + [SMEM] * gated
    shape = (count,) + acc.shape[1:]
    out = call(
        functools.partial(newton_kernel, count, first, offset, extra, gated),
        "newton",
        (jax.ShapeDtypeStruct(shape, bf16),) + ((jax.ShapeDtypeStruct(shape, f32),) if gated else ()),
        specs,
        (VMEM,) * (1 + gated),
        args,
        moved=moved,
        scratch=[] if gated else [pltpu.VMEM((8, 128), f32)],
    )
    return out if gated else out[0]


def newton_rest_kernel(others, chip, *refs):
    out = refs[-1]
    grams = []
    for i in range(chip.shape[0]):
        g = chip[i]
        for other in refs[:others]:
            g = g + other[i].astype(f32)
        grams.append(g)
    polar(grams, out)


def leading_kernel(same, residual, own, sibling, out):
    for b in range(MOVE):
        rotation = jnp.where(same[b, :1] > 0.5, own[0], sibling[0])
        out[b] = jnp.dot(residual[b], rotation, preferred_element_type=f32).astype(bf16)


def pair_kernel(near, far, out):
    out[0] = near[...]
    out[1] = far[...]


def arrived_kernel(*refs):
    refs[-1][...] = jnp.zeros_like(refs[-1])


def gather_kernel(starts, n_own, *refs):
    owns, siblings, rots = refs[:n_own], refs[n_own:-1], refs[-1]
    core = lax.rem(lax.axis_index("narrow"), CORES)
    for s, own in zip(starts, owns):
        for i in range(own.shape[0]):
            rots[CORES * (s + i) + core] = own[i]
    for s, sibling in zip(starts, siblings):
        for i in range(sibling.shape[0]):
            rots[CORES * (s + i) + 1 - core] = sibling[i]


def turn_kernel(first, hops, plan_hbm, residual, main, _, *refs):
    parts = refs[:len(hops)]
    out, rots, plan, turned, sems, plan_sem = refs[-6:]
    blocks, rows, _ = residual.shape
    piece = blocks // PIECES
    core = lax.rem(lax.axis_index("narrow"), CORES)
    here = lax.axis_index("wide")
    fetch = pltpu.make_async_copy(plan_hbm, plan, plan_sem)
    fetch.start()
    for i in range(main.shape[0]):
        rots[CORES * (first + i) + 1 - core] = main[i]
    fetch.wait()
    copies = []
    for i in reversed(range(PIECES)):
        for b in reversed(range(i * piece, (i + 1) * piece)):
            if b >= MOVE:
                turned[b] = jnp.dot(residual[b], rots[plan[b]], preferred_element_type=f32).astype(bf16)
                continue
            donor = plan[blocks + 1 + b]
            picked = parts[0][0, b]
            for part, group in zip(parts, hops):
                for k, hop in enumerate(group):
                    match = donor == (hop if len(parts) == 1 else here ^ hop)
                    picked = jnp.where(match, part[k, b], picked)
            turned[b] = picked
        at = pl.ds(i * piece, piece)
        copies.append(pltpu.make_async_copy(turned.at[at], out.at[at], sems.at[i]))
        copies[-1].start()
    for copy in copies:
        copy.wait()


def turn_rest_kernel(first, bl, ln, plan, own, sibling, centroids, points_hbm, _, out, block):
    blocks, rows, _ = points_hbm.shape
    me = lax.axis_index("narrow")
    core = lax.rem(me, CORES)
    row_ids = lax.broadcasted_iota(i32, block.shape, 0) + me * rows

    @pl.loop(MOVE, blocks)
    def _(b):
        @pl.when(plan[b] >= first)
        def _():
            pltpu.sync_copy(points_hbm.at[b], block)
            kept = row_ids < ln[b]
            residual = jnp.where(kept, block[...].astype(f32) - centroids[pl.ds(bl[b], 1), :], 0.0).astype(bf16)
            at = lax.div(plan[b] - first, CORES)
            mine = lax.rem(plan[b], CORES) == core
            rotation = jnp.where(mine, own[at], sibling[at])
            block[...] = jnp.dot(residual, rotation, preferred_element_type=f32).astype(bf16)
            pltpu.sync_copy(block, out.at[b])


def pieces_of(count):
    return [count]


def local(wide, narrow, points, targets, centroids, block_list, lengths, sources):
    blocks, rows, width = points.shape
    lists = centroids.shape[0]
    per = lists // CORES
    chips = narrow // CORES
    mat = (width, width)
    lead = MOVE // CORES
    cap = per * 3 // 4 if chips == 2 else per
    rest = per - cap

    plan, crossing, residual, same, acc, send = call(
        gram_kernel,
        "grams",
        (
            jax.ShapeDtypeStruct((blocks + 1 + MOVE,), i32),
            jax.ShapeDtypeStruct((1,), i32),
            jax.ShapeDtypeStruct(points.shape, bf16),
            jax.ShapeDtypeStruct((MOVE, 8, width), f32),
            jax.ShapeDtypeStruct((lists,) + mat, f32),
            jax.ShapeDtypeStruct((lead,) + mat, bf16),
        ),
        [HBM] * 6,
        (SMEM, SMEM, VMEM, VMEM, VMEM, VMEM),
        tuple(stay(x) for x in (block_list, lengths, sources, points, targets, centroids)),
        scratch=[
            pltpu.SMEM((blocks,), i32),
            pltpu.SMEM((blocks,), i32),
            pltpu.SMEM((blocks,), i32),
            pltpu.SMEM((lists,), i32),
            pltpu.VMEM(points.shape, bf16),
            pltpu.VMEM(points.shape, bf16),
            pltpu.VMEM(centroids.shape, f32),
            pltpu.SemaphoreType.DMA((2, PIECES)),
            pltpu.SemaphoreType.DMA((4,)),
        ],
    )

    to_core = [(i, i ^ 1) for i in range(narrow)]
    to_chip = [[(i, (i + CORES * k) % narrow) for i in range(narrow)] for k in range(1, chips)]

    def cross(part):
        return tuple(lax.ppermute(part, "narrow", perm) for perm in to_chip)

    def swap(part):
        return lax.ppermute(part, "narrow", to_core)

    recv = swap(send)
    lead_chip, send_others = call(
        functools.partial(lead_sum_kernel, per),
        "lead_sum",
        (jax.ShapeDtypeStruct((lead,) + mat, bf16), jax.ShapeDtypeStruct((per - lead,) + mat, bf16)),
        [VMEM, VMEM],
        (VMEM, VMEM),
        (acc, recv),
    )
    lead_crossed = cross(lead_chip)
    recv_others = swap(send_others)

    def chip_sums(counts):
        return call(
            functools.partial(sum_kernel, lead),
            "chip_sums",
            tuple(jax.ShapeDtypeStruct((count,) + mat, bf16) for count in counts),
            [VMEM, VMEM],
            (VMEM,) * len(counts),
            (acc, recv_others),
        )

    main_chips = chip_sums(pieces_of(cap - lead))
    main_crossed = [cross(part) for part in main_chips]
    tokens = main_chips
    starts, owns = [0], []
    if rest:
        starts.append(cap)
        overflow = crossing[0] > CORES * cap
        tokens = (*tokens, overflow.astype(i32).reshape(1))
        rest_own, rest_chip = newton(acc, cap, rest, recv_others, cap - lead, (), tokens, plan, 1 << 12)
        owns.append(rest_own)
        tokens = (rest_own,)
    owns.insert(0, newton(acc, 0, lead, recv, 0, (lead_crossed,), tokens))
    siblings = [swap(owns[0])]

    leading = call(
        leading_kernel,
        "turn_leading",
        jax.ShapeDtypeStruct((MOVE, rows, width), bf16),
        [VMEM] * 4,
        VMEM,
        (same, residual, owns[0], siblings[0]),
        flops=LEAD_FLOPS,
    )
    if wide <= 16 and wide & (wide - 1) == 0:
        half = wide // 2
        far = lax.ppermute(leading, "wide", [(i, i ^ half) for i in range(wide)])
        pair = call(
            pair_kernel,
            "pair",
            jax.ShapeDtypeStruct((2,) + leading.shape, bf16),
            [VMEM, VMEM],
            VMEM,
            (leading, far),
            flops=PAIR_FLOPS,
        )
        order = range(1, half)
        parts = [pair] + [lax.ppermute(pair, "wide", [(i, i ^ k) for i in range(wide)]) for k in order]
        hops = [(k, k ^ half) for k in [0, *order]]
        token = pair
    else:
        parts = [lax.all_gather(leading, "wide", axis=0)]
        hops = [tuple(range(wide))]
        token = leading
    main = newton(acc, lead, cap - lead, recv_others, 0, main_crossed, (token,))
    siblings += [swap(own) for own in owns[1:]]
    other = swap(main)

    rots = call(
        functools.partial(gather_kernel, starts + [lead], len(owns) + 1),
        "gather_rotations",
        jax.ShapeDtypeStruct((lists,) + mat, bf16),
        [VMEM] * (1 + len(owns) + len(siblings)),
        VMEM,
        (*owns, main, *siblings),
    )
    token = call(
        arrived_kernel,
        "arrived",
        jax.ShapeDtypeStruct((8, 128), f32),
        [ANY] * (1 + len(parts)),
        VMEM,
        (*parts, rots),
        moved=LONG,
    )
    turned, _ = call(
        functools.partial(turn_kernel, lead, hops),
        "turn",
        (pltpu.HBM(points.shape, bf16), jax.ShapeDtypeStruct(rots.shape, bf16)),
        [ANY] + [VMEM] * (3 + len(parts)) + [ANY],
        (HBM, VMEM),
        (plan, residual, other, rots, *parts, token),
        scratch=[
            pltpu.SMEM(plan.shape, i32),
            pltpu.VMEM(points.shape, bf16),
            pltpu.SemaphoreType.DMA((PIECES,)),
            pltpu.SemaphoreType.DMA(()),
        ],
        aliases={3: 1},
    )
    if not rest:
        return turned

    def exchange_rest(state):
        turned, chip = state
        own = call(
            functools.partial(newton_rest_kernel, len(to_chip)),
            "newton_rest",
            jax.ShapeDtypeStruct(chip.shape, bf16),
            [VMEM] * (1 + len(to_chip)),
            VMEM,
            (chip, *cross(chip.astype(bf16))),
        )
        turned = call(
            functools.partial(turn_rest_kernel, CORES * cap),
            "turn_rest",
            pltpu.HBM(turned.shape, bf16),
            [SMEM] * 3 + [VMEM] * 3 + [HBM] * 2,
            HBM,
            (block_list, lengths, plan, own, swap(own), centroids, stay(points), stay(turned)),
            scratch=[pltpu.VMEM((rows, width), bf16)],
            aliases={7: 0},
        )
        return turned

    return lax.cond(overflow, exchange_rest, lambda state: state[0], (turned, rest_chip))


def solution(mesh):
    return jax.shard_map(
        functools.partial(local, mesh.shape["wide"], mesh.shape["narrow"]),
        mesh=mesh,
        in_specs=(
            P("wide", "narrow", None),
            P("wide", "narrow", None),
            P("wide", None),
            P("wide"),
            P("wide"),
            P("wide"),
        ),
        out_specs=P("wide", "narrow", None),
        check_vma=False,
    )
```

```python
import functools

import jax
import jax.numpy as jnp
from jax import lax
from jax.experimental import pallas as pl
from jax.experimental.pallas import tpu as pltpu
from jax.sharding import PartitionSpec as P

MOVE = 2
ITERS = 5
CORES = 2
PIECES = 2
STORES = 8
VMEM_LIMIT = 14 * 1024 * 1024
LONG = 1 << 30
GROUP = 4
LEAD_FLOPS = 2800000000
PAIR_FLOPS = 0

f32, bf16, i32 = jnp.float32, jnp.bfloat16, jnp.int32

SMEM = pl.BlockSpec(memory_space=pltpu.SMEM)
VMEM = pl.BlockSpec(memory_space=pltpu.VMEM)
HBM = pl.BlockSpec(memory_space=pltpu.HBM)
ANY = pl.BlockSpec(memory_space=pl.ANY)


def stay(x):
    return pltpu.with_memory_space_constraint(x, pltpu.HBM)


def call(kernel, name, outs, in_specs, out_specs, args, moved=1 << 20, flops=0, scratch=(), aliases={}):
    return pl.pallas_call(
        kernel,
        out_shape=outs,
        in_specs=in_specs,
        out_specs=out_specs,
        scratch_shapes=scratch,
        input_output_aliases=aliases,
        compiler_params=pltpu.CompilerParams(vmem_limit_bytes=VMEM_LIMIT),
        cost_estimate=pl.CostEstimate(flops=16 * moved if moved == LONG else flops, bytes_accessed=moved, transcendentals=0),
        name=name,
    )(*args)


def assign_slots(bl, ln, first_rows, slot_of_list, plan):
    blocks, lists = bl.shape[0], slot_of_list.shape[0]
    for l in range(lists):
        slot_of_list[l] = -1

    def visit(b, nxt, wanted):
        l = bl[b]
        s = slot_of_list[l]
        new = jnp.logical_and(s < 0, wanted)
        slot_of_list[l] = jnp.where(new, nxt, s)
        return nxt + new.astype(i32)

    nxt = jnp.int32(0)
    for b in range(MOVE):
        nxt = visit(b, nxt, True)
    for b in range(MOVE, blocks):
        nxt = visit(b, nxt, ln[b] > first_rows)
    plan[blocks + 1 + MOVE] = nxt
    for b in range(MOVE, blocks):
        nxt = visit(b, nxt, True)
    plan[blocks] = nxt
    for b in range(blocks):
        plan[b] = slot_of_list[bl[b]]


def gram_kernel(bl_hbm, ln_hbm, sources_hbm, points_hbm, targets_hbm, centroids_hbm, table, residual, same, acc, send, *scratch):
    bl, ln, sources, slot_of_list, plan, points, targets, centroids, sems, int_sems = scratch
    blocks, rows, _ = points.shape
    per = acc.shape[0] // CORES
    piece = blocks // PIECES
    copies = [
        pltpu.make_async_copy(bl_hbm, bl, int_sems.at[0]),
        pltpu.make_async_copy(ln_hbm, ln, int_sems.at[1]),
        pltpu.make_async_copy(centroids_hbm, centroids, int_sems.at[2]),
        pltpu.make_async_copy(sources_hbm, sources, int_sems.at[3]),
    ]
    for copy in copies:
        copy.start()
    parts = []
    for i in range(PIECES):
        at = pl.ds(i * piece, piece)
        pair = (
            pltpu.make_async_copy(points_hbm.at[at], points.at[at], sems.at[0, i]),
            pltpu.make_async_copy(targets_hbm.at[at], targets.at[at], sems.at[1, i]),
        )
        for copy in pair:
            copy.start()
        parts.append(pair)
    me = lax.axis_index("narrow")
    core = lax.rem(me, CORES)
    acc[...] = jnp.zeros_like(acc)
    copies[0].wait()
    copies[1].wait()
    assign_slots(bl, ln, CORES * rows, slot_of_list, plan)
    copies[2].wait()
    copies[3].wait()
    for j in range(MOVE):
        plan[blocks + 1 + j] = lax.div(sources[j], blocks)
        mine = lax.rem(plan[j], CORES) == core
        same[j] = jnp.full(same.shape[1:], jnp.where(mine, 1.0, 0.0), f32)
    lanes = lax.broadcasted_iota(i32, table.shape, 1)
    entries = jnp.zeros(table.shape, i32)
    for k in range(plan.shape[0]):
        entries = jnp.where(lanes == k, plan[k], entries)
    table[...] = entries
    row_ids = lax.broadcasted_iota(i32, points.shape[1:], 0) + me * rows
    for i in range(PIECES):
        for copy in parts[i]:
            copy.wait()
        for b in range(i * piece, (i + 1) * piece):
            kept = row_ids < ln[b]
            res = jnp.where(kept, points[b].astype(f32) - centroids[pl.ds(bl[b], 1), :], 0.0).astype(bf16)
            residual[b] = res
            slot = plan[b]
            at = lax.div(slot, CORES) + jnp.where(lax.rem(slot, CORES) == core, 0, per)
            acc[at] += lax.dot_general(res, targets[b], (((0,), (0,)), ((), ())), preferred_element_type=f32)
    for i in range(send.shape[0]):
        send[i] = acc[per + i].astype(bf16)


def lead_sum_kernel(per, acc, recv, chip, send):
    lead = recv.shape[0]
    chip[...] = (acc[:lead] + recv[...].astype(f32)).astype(bf16)
    for i in range(send.shape[0]):
        send[i] = acc[per + lead + i].astype(bf16)


def sum_kernel(first, acc, recv, *sums):
    at = 0
    for out in sums:
        count = out.shape[0]
        out[...] = (acc[first + at:first + at + count] + recv[at:at + count].astype(f32)).astype(bf16)
        at += count


def newton_kernel(count, first, offset, extra, gated, acc, recv, *refs):
    pieces, out, chip = refs[:-2], refs[-2], refs[-1]

    def run():
        xs = []
        for i in range(count):
            g = acc[first + i] + recv[offset + i].astype(f32)
            if gated:
                chip[i] = g
            for which in extra:
                piece, row = which[i]
                g = g + pieces[piece][row].astype(f32)
            xs.append(g)
        polar(xs, out)

    if not gated:
        run()
    else:
        used = refs[-3][0, gated] > CORES * first
        pl.when(used)(run)

        @pl.when(jnp.logical_not(used))
        def _():
            out[...] = jnp.zeros_like(out)
            chip[...] = jnp.zeros_like(chip)


def polar(grams, out):
    xs = []
    for g in grams:
        gb = g.astype(bf16)
        p = lax.dot_general(gb, gb, (((1,), (1,)), ((), ())), preferred_element_type=f32)
        scale = lax.rsqrt(jnp.sum(g * g) + 1e-6)
        p = (p * (scale * scale)).astype(bf16)
        xs.append((1.5 * scale) * g - (0.5 * scale) * jnp.dot(p, gb, preferred_element_type=f32))
    for _ in range(ITERS - 1):
        for i, x in enumerate(xs):
            xb = x.astype(bf16)
            p = lax.dot_general(xb, xb, (((1,), (1,)), ((), ())), preferred_element_type=f32).astype(bf16)
            xs[i] = 1.5 * x - 0.5 * jnp.dot(p, xb, preferred_element_type=f32)
    for i, x in enumerate(xs):
        out[i] = x.astype(bf16)


def newton(acc, first, count, recv, offset, crossed, after=(), table=None, at=0, moved=1 << 20):
    extra = [[] for _ in (crossed[0] if crossed else ())]
    flat = []
    for group in crossed:
        for chip, part in enumerate(group):
            extra[chip] += [(len(flat), row) for row in range(part.shape[0])]
            flat.append(part)
    gated = table is not None
    args = (acc, recv, *flat, *after) + ((table,) if gated else ())
    specs = [VMEM] * (2 + len(flat)) + [ANY] * len(after) + [VMEM] * gated
    shape = (count,) + acc.shape[1:]
    out = call(
        functools.partial(newton_kernel, count, first, offset, extra, at if gated else 0),
        "newton",
        (jax.ShapeDtypeStruct(shape, bf16),) + ((jax.ShapeDtypeStruct(shape, f32),) if gated else ()),
        specs,
        (VMEM,) * (1 + gated),
        args,
        moved=moved,
        scratch=[] if gated else [pltpu.VMEM((8, 128), f32)],
    )
    return out if gated else out[0]


def newton_rest_kernel(others, chip, *refs):
    out = refs[-1]
    grams = []
    for i in range(chip.shape[0]):
        g = chip[i]
        for other in refs[:others]:
            g = g + other[i].astype(f32)
        grams.append(g)
    polar(grams, out)


def leading_kernel(same, residual, own, sibling, out):
    for b in range(MOVE):
        rotation = jnp.where(same[b, :1] > 0.5, own[0], sibling[0])
        out[b] = jnp.dot(residual[b], rotation, preferred_element_type=f32).astype(bf16)


def pair_kernel(near, far, out):
    out[0] = near[...]
    out[1] = far[...]


def arrived_kernel(*refs):
    refs[-1][...] = jnp.zeros_like(refs[-1])


def gather_kernel(starts, n_own, *refs):
    owns, siblings, rots = refs[:n_own], refs[n_own:-1], refs[-1]
    core = lax.rem(lax.axis_index("narrow"), CORES)
    for s, own in zip(starts, owns):
        for i in range(own.shape[0]):
            rots[CORES * (s + i) + core] = own[i]
    for s, sibling in zip(starts, siblings):
        for i in range(sibling.shape[0]):
            rots[CORES * (s + i) + 1 - core] = sibling[i]


def turn_kernel(first, hops, table, residual, main, _, *refs):
    parts = refs[:len(hops)]
    out, rots, turned, sems = refs[-4:]
    blocks, rows, _ = residual.shape
    piece = blocks // STORES
    core = lax.rem(lax.axis_index("narrow"), CORES)
    here = lax.axis_index("wide")
    plan = table[...]
    for i in range(main.shape[0]):
        rots[CORES * (first + i) + 1 - core] = main[i]
    copies = []
    for i in reversed(range(STORES)):
        for b in reversed(range(i * piece, (i + 1) * piece)):
            if b >= MOVE:
                turned[b] = jnp.dot(residual[b], rots[plan[0, b]], preferred_element_type=f32).astype(bf16)
                continue
            donor = plan[0, blocks + 1 + b]
            picked = parts[0][0, b]
            for part, group in zip(parts, hops):
                for k, hop in enumerate(group):
                    match = donor == (hop if len(parts) == 1 else here ^ hop)
                    picked = jnp.where(match, part[k, b], picked)
            turned[b] = picked
        at = pl.ds(i * piece, piece)
        copies.append(pltpu.make_async_copy(turned.at[at], out.at[at], sems.at[i]))
        copies[-1].start()
    for copy in copies:
        copy.wait()


def turn_rest_kernel(first, bl, ln, plan, own, sibling, centroids, points_hbm, _, out, block):
    blocks, rows, _ = points_hbm.shape
    me = lax.axis_index("narrow")
    core = lax.rem(me, CORES)
    row_ids = lax.broadcasted_iota(i32, block.shape, 0) + me * rows

    @pl.loop(MOVE, blocks)
    def _(b):
        @pl.when(plan[b] >= first)
        def _():
            pltpu.sync_copy(points_hbm.at[b], block)
            kept = row_ids < ln[b]
            residual = jnp.where(kept, block[...].astype(f32) - centroids[pl.ds(bl[b], 1), :], 0.0).astype(bf16)
            at = lax.div(plan[b] - first, CORES)
            mine = lax.rem(plan[b], CORES) == core
            rotation = jnp.where(mine, own[at], sibling[at])
            block[...] = jnp.dot(residual, rotation, preferred_element_type=f32).astype(bf16)
            pltpu.sync_copy(block, out.at[b])


def pieces_of(count):
    return [count]


def local(wide, narrow, points, targets, centroids, block_list, lengths, sources):
    blocks, rows, width = points.shape
    lists = centroids.shape[0]
    per = lists // CORES
    chips = narrow // CORES
    mat = (width, width)
    lead = MOVE // CORES
    cap = per * 3 // 4 if chips == 2 else per
    rest = per - cap

    entries = blocks + 2 + MOVE
    table, residual, same, acc, send = call(
        gram_kernel,
        "grams",
        (
            jax.ShapeDtypeStruct((8, -(-entries // 128) * 128), i32),
            jax.ShapeDtypeStruct(points.shape, bf16),
            jax.ShapeDtypeStruct((MOVE, 8, width), f32),
            jax.ShapeDtypeStruct((lists,) + mat, f32),
            jax.ShapeDtypeStruct((lead,) + mat, bf16),
        ),
        [HBM] * 6,
        (VMEM,) * 5,
        tuple(stay(x) for x in (block_list, lengths, sources, points, targets, centroids)),
        scratch=[
            pltpu.SMEM((blocks,), i32),
            pltpu.SMEM((blocks,), i32),
            pltpu.SMEM((blocks,), i32),
            pltpu.SMEM((lists,), i32),
            pltpu.SMEM((entries,), i32),
            pltpu.VMEM(points.shape, bf16),
            pltpu.VMEM(points.shape, bf16),
            pltpu.VMEM(centroids.shape, f32),
            pltpu.SemaphoreType.DMA((2, PIECES)),
            pltpu.SemaphoreType.DMA((4,)),
        ],
    )

    to_core = [(i, i ^ 1) for i in range(narrow)]
    to_chip = [[(i, (i + CORES * k) % narrow) for i in range(narrow)] for k in range(1, chips)]

    def cross(part):
        return tuple(lax.ppermute(part, "narrow", perm) for perm in to_chip)

    def swap(part):
        return lax.ppermute(part, "narrow", to_core)

    recv = swap(send)
    lead_chip, send_others = call(
        functools.partial(lead_sum_kernel, per),
        "lead_sum",
        (jax.ShapeDtypeStruct((lead,) + mat, bf16), jax.ShapeDtypeStruct((per - lead,) + mat, bf16)),
        [VMEM, VMEM],
        (VMEM, VMEM),
        (acc, recv),
    )
    lead_crossed = cross(lead_chip)
    recv_others = swap(send_others)

    def chip_sums(counts):
        return call(
            functools.partial(sum_kernel, lead),
            "chip_sums",
            tuple(jax.ShapeDtypeStruct((count,) + mat, bf16) for count in counts),
            [VMEM, VMEM],
            (VMEM,) * len(counts),
            (acc, recv_others),
        )

    main_chips = chip_sums(pieces_of(cap - lead))
    main_crossed = [cross(part) for part in main_chips]
    tokens = main_chips
    starts, owns = [0], []
    if rest:
        starts.append(cap)
        overflow = table[0, entries - 1] > CORES * cap
        tokens = (*tokens, overflow.astype(i32).reshape(1))
        rest_own, rest_chip = newton(acc, cap, rest, recv_others, cap - lead, (), tokens, table, blocks, 1 << 12)
        owns.append(rest_own)
        tokens = (rest_own,)
    owns.insert(0, newton(acc, 0, lead, recv, 0, (lead_crossed,), tokens))
    siblings = [swap(owns[0])]

    leading = call(
        leading_kernel,
        "turn_leading",
        jax.ShapeDtypeStruct((MOVE, rows, width), bf16),
        [VMEM] * 4,
        VMEM,
        (same, residual, owns[0], siblings[0]),
        flops=LEAD_FLOPS,
    )
    if wide <= 16 and wide & (wide - 1) == 0:
        half = wide // 2
        far = lax.ppermute(leading, "wide", [(i, i ^ half) for i in range(wide)])
        pair = call(
            pair_kernel,
            "pair",
            jax.ShapeDtypeStruct((2,) + leading.shape, bf16),
            [VMEM, VMEM],
            VMEM,
            (leading, far),
            flops=PAIR_FLOPS,
        )
        order = range(1, half)
        parts = [pair] + [lax.ppermute(pair, "wide", [(i, i ^ k) for i in range(wide)]) for k in order]
        hops = [(k, k ^ half) for k in [0, *order]]
        token = pair
    else:
        parts = [lax.all_gather(leading, "wide", axis=0)]
        hops = [tuple(range(wide))]
        token = leading
    main = newton(acc, lead, cap - lead, recv_others, 0, main_crossed, (token,))
    siblings += [swap(own) for own in owns[1:]]
    other = swap(main)

    rots = call(
        functools.partial(gather_kernel, starts + [lead], len(owns) + 1),
        "gather_rotations",
        jax.ShapeDtypeStruct((lists,) + mat, bf16),
        [VMEM] * (1 + len(owns) + len(siblings)),
        VMEM,
        (*owns, main, *siblings),
    )
    token = call(
        arrived_kernel,
        "arrived",
        jax.ShapeDtypeStruct((8, 128), f32),
        [ANY] * (1 + len(parts)),
        VMEM,
        (*parts, rots),
        moved=LONG,
    )
    turned, _ = call(
        functools.partial(turn_kernel, lead, hops),
        "turn",
        (pltpu.HBM(points.shape, bf16), jax.ShapeDtypeStruct(rots.shape, bf16)),
        [VMEM] * (4 + len(parts)) + [ANY],
        (HBM, VMEM),
        (table, residual, other, rots, *parts, token),
        scratch=[
            pltpu.VMEM(points.shape, bf16),
            pltpu.SemaphoreType.DMA((STORES,)),
        ],
        aliases={3: 1},
    )
    if not rest:
        return turned

    def exchange_rest(state):
        turned, chip = state
        own = call(
            functools.partial(newton_rest_kernel, len(to_chip)),
            "newton_rest",
            jax.ShapeDtypeStruct(chip.shape, bf16),
            [VMEM] * (1 + len(to_chip)),
            VMEM,
            (chip, *cross(chip.astype(bf16))),
        )
        turned = call(
            functools.partial(turn_rest_kernel, CORES * cap),
            "turn_rest",
            pltpu.HBM(turned.shape, bf16),
            [SMEM] * 3 + [VMEM] * 3 + [HBM] * 2,
            HBM,
            (block_list, lengths, table[0, :blocks], own, swap(own), centroids, stay(points), stay(turned)),
            scratch=[pltpu.VMEM((rows, width), bf16)],
            aliases={7: 0},
        )
        return turned

    return lax.cond(overflow, exchange_rest, lambda state: state[0], (turned, rest_chip))


def solution(mesh):
    return jax.shard_map(
        functools.partial(local, mesh.shape["wide"], mesh.shape["narrow"]),
        mesh=mesh,
        in_specs=(
            P("wide", "narrow", None),
            P("wide", "narrow", None),
            P("wide", None),
            P("wide"),
            P("wide"),
            P("wide"),
        ),
        out_specs=P("wide", "narrow", None),
        check_vma=False,
    )
```

```python
import functools

import jax
import jax.numpy as jnp
from jax import lax
from jax.experimental import pallas as pl
from jax.experimental.pallas import tpu as pltpu
from jax.sharding import PartitionSpec as P

MOVE = 2
ITERS = 5
CORES = 2
PIECES = 2
STORES = 8
VMEM_LIMIT = 14 * 1024 * 1024
LONG = 1 << 30
GROUP = 4
LEAD_FLOPS = 1350000000
PAIR_FLOPS = 1500000000

f32, bf16, i32 = jnp.float32, jnp.bfloat16, jnp.int32

SMEM = pl.BlockSpec(memory_space=pltpu.SMEM)
VMEM = pl.BlockSpec(memory_space=pltpu.VMEM)
HBM = pl.BlockSpec(memory_space=pltpu.HBM)
ANY = pl.BlockSpec(memory_space=pl.ANY)


def stay(x):
    return pltpu.with_memory_space_constraint(x, pltpu.HBM)


def call(kernel, name, outs, in_specs, out_specs, args, moved=1 << 20, flops=0, scratch=(), aliases={}):
    return pl.pallas_call(
        kernel,
        out_shape=outs,
        in_specs=in_specs,
        out_specs=out_specs,
        scratch_shapes=scratch,
        input_output_aliases=aliases,
        compiler_params=pltpu.CompilerParams(vmem_limit_bytes=VMEM_LIMIT),
        cost_estimate=pl.CostEstimate(flops=16 * moved if moved == LONG else flops, bytes_accessed=moved, transcendentals=0),
        name=name,
    )(*args)


def assign_slots(bl, ln, first_rows, slot_of_list, plan):
    blocks, lists = bl.shape[0], slot_of_list.shape[0]
    for l in range(lists):
        slot_of_list[l] = -1

    def visit(b, nxt, wanted):
        l = bl[b]
        s = slot_of_list[l]
        new = jnp.logical_and(s < 0, wanted)
        slot_of_list[l] = jnp.where(new, nxt, s)
        return nxt + new.astype(i32)

    nxt = jnp.int32(0)
    for b in range(MOVE):
        nxt = visit(b, nxt, True)
    for b in range(MOVE, blocks):
        nxt = visit(b, nxt, ln[b] > first_rows)
    plan[blocks + 1 + MOVE] = nxt
    for b in range(MOVE, blocks):
        nxt = visit(b, nxt, True)
    plan[blocks] = nxt
    for b in range(blocks):
        plan[b] = slot_of_list[bl[b]]


def gram_kernel(bl_hbm, ln_hbm, sources_hbm, points_hbm, targets_hbm, centroids_hbm, table, residual, same, acc, send, *scratch):
    bl, ln, sources, slot_of_list, plan, points, targets, centroids, sems, int_sems = scratch
    blocks, rows, _ = points.shape
    per = acc.shape[0] // CORES
    piece = blocks // PIECES
    copies = [
        pltpu.make_async_copy(bl_hbm, bl, int_sems.at[0]),
        pltpu.make_async_copy(ln_hbm, ln, int_sems.at[1]),
        pltpu.make_async_copy(centroids_hbm, centroids, int_sems.at[2]),
        pltpu.make_async_copy(sources_hbm, sources, int_sems.at[3]),
    ]
    for copy in copies:
        copy.start()
    parts = []
    for i in range(PIECES):
        at = pl.ds(i * piece, piece)
        pair = (
            pltpu.make_async_copy(points_hbm.at[at], points.at[at], sems.at[0, i]),
            pltpu.make_async_copy(targets_hbm.at[at], targets.at[at], sems.at[1, i]),
        )
        for copy in pair:
            copy.start()
        parts.append(pair)
    me = lax.axis_index("narrow")
    core = lax.rem(me, CORES)
    acc[...] = jnp.zeros_like(acc)
    copies[0].wait()
    copies[1].wait()
    assign_slots(bl, ln, CORES * rows, slot_of_list, plan)
    copies[2].wait()
    copies[3].wait()
    for j in range(MOVE):
        plan[blocks + 1 + j] = lax.div(sources[j], blocks)
        mine = lax.rem(plan[j], CORES) == core
        same[j] = jnp.full(same.shape[1:], jnp.where(mine, 1.0, 0.0), f32)
    lanes = lax.broadcasted_iota(i32, table.shape, 1)
    entries = jnp.zeros(table.shape, i32)
    for k in range(plan.shape[0]):
        entries = jnp.where(lanes == k, plan[k], entries)
    table[...] = entries
    row_ids = lax.broadcasted_iota(i32, points.shape[1:], 0) + me * rows
    for i in range(PIECES):
        for copy in parts[i]:
            copy.wait()
        for b in range(i * piece, (i + 1) * piece):
            kept = row_ids < ln[b]
            res = jnp.where(kept, points[b].astype(f32) - centroids[pl.ds(bl[b], 1), :], 0.0).astype(bf16)
            residual[b] = res
            slot = plan[b]
            at = lax.div(slot, CORES) + jnp.where(lax.rem(slot, CORES) == core, 0, per)
            acc[at] += lax.dot_general(res, targets[b], (((0,), (0,)), ((), ())), preferred_element_type=f32)
    for i in range(send.shape[0]):
        send[i] = acc[per + i].astype(bf16)


def lead_sum_kernel(per, acc, recv, chip, *sends):
    at = chip.shape[0]
    chip[...] = (acc[:at] + recv[...].astype(f32)).astype(bf16)
    for out in sends:
        count = out.shape[0]
        out[...] = acc[per + at:per + at + count].astype(bf16)
        at += count


def table_kernel(table, _, out):
    out[...] = table[...]


def sum_kernel(first, acc, recv, *refs):
    out = refs[-1]
    count = out.shape[0]
    out[...] = (acc[first:first + count] + recv[...].astype(f32)).astype(bf16)


def newton_kernel(count, first, offset, extra, keep, acc, recv, *refs):
    pieces, out, chip = refs[:-2], refs[-2], refs[-1]
    grams = []
    for i in range(count):
        g = acc[first + i] + recv[offset + i].astype(f32)
        if keep:
            chip[i] = g
        for which in extra:
            piece, row = which[i]
            g = g + pieces[piece][row].astype(f32)
        grams.append(g)
    polar(grams, out)


def polar(grams, out):
    xs = []
    for g in grams:
        gb = g.astype(bf16)
        p = lax.dot_general(gb, gb, (((1,), (1,)), ((), ())), preferred_element_type=f32)
        scale = lax.rsqrt(jnp.sum(g * g) + 1e-6)
        p = (p * (scale * scale)).astype(bf16)
        xs.append((1.5 * scale) * g - (0.5 * scale) * jnp.dot(p, gb, preferred_element_type=f32))
    for _ in range(ITERS - 1):
        for i, x in enumerate(xs):
            xb = x.astype(bf16)
            p = lax.dot_general(xb, xb, (((1,), (1,)), ((), ())), preferred_element_type=f32).astype(bf16)
            xs[i] = 1.5 * x - 0.5 * jnp.dot(p, xb, preferred_element_type=f32)
    for i, x in enumerate(xs):
        out[i] = x.astype(bf16)


def newton(acc, first, count, recv, offset, crossed, after=(), keep=False, moved=1 << 20):
    extra = [[] for _ in (crossed[0] if crossed else ())]
    flat = []
    for group in crossed:
        for chip, part in enumerate(group):
            extra[chip] += [(len(flat), row) for row in range(part.shape[0])]
            flat.append(part)
    shape = (count,) + acc.shape[1:]
    out = call(
        functools.partial(newton_kernel, count, first, offset, extra, keep),
        "newton",
        (jax.ShapeDtypeStruct(shape, bf16),) + ((jax.ShapeDtypeStruct(shape, f32),) if keep else ()),
        [VMEM] * (2 + len(flat)) + [ANY] * len(after),
        (VMEM,) * (1 + keep),
        (acc, recv, *flat, *after),
        moved=moved,
        scratch=[] if keep else [pltpu.VMEM((8, 128), f32)],
    )
    return out if keep else out[0]


def newton_rest_kernel(others, chip, *refs):
    out = refs[-1]
    grams = []
    for i in range(chip.shape[0]):
        g = chip[i]
        for other in refs[:others]:
            g = g + other[i].astype(f32)
        grams.append(g)
    polar(grams, out)


def leading_kernel(same, residual, own, sibling, out):
    for b in range(MOVE):
        rotation = jnp.where(same[b, :1] > 0.5, own[0], sibling[0])
        out[b] = jnp.dot(residual[b], rotation, preferred_element_type=f32).astype(bf16)


def pair_kernel(near, far, *refs):
    out = refs[-1]
    out[0] = near[...]
    out[1] = far[...]


def arrived_kernel(*refs):
    refs[-1][...] = jnp.zeros_like(refs[-1])


def gather_kernel(starts, n_own, *refs):
    owns, siblings, rots = refs[:n_own], refs[n_own:-1], refs[-1]
    core = lax.rem(lax.axis_index("narrow"), CORES)
    for s, own in zip(starts, owns):
        for i in range(own.shape[0]):
            rots[CORES * (s + i) + core] = own[i]
    for s, sibling in zip(starts, siblings):
        for i in range(sibling.shape[0]):
            rots[CORES * (s + i) + 1 - core] = sibling[i]


def turn_kernel(first, hops, table, residual, main, _, *refs):
    parts = refs[:len(hops)]
    out, rots, turned, sems = refs[-4:]
    blocks, rows, _ = residual.shape
    piece = blocks // STORES
    core = lax.rem(lax.axis_index("narrow"), CORES)
    here = lax.axis_index("wide")
    plan = table[...]
    for i in range(main.shape[0]):
        rots[CORES * (first + i) + 1 - core] = main[i]
    copies = []
    for i in reversed(range(STORES)):
        for b in reversed(range(i * piece, (i + 1) * piece)):
            if b >= MOVE:
                turned[b] = jnp.dot(residual[b], rots[plan[0, b]], preferred_element_type=f32).astype(bf16)
                continue
            donor = plan[0, blocks + 1 + b]
            picked = parts[0][0, b]
            for part, group in zip(parts, hops):
                for k, hop in enumerate(group):
                    match = donor == (hop if len(parts) == 1 else here ^ hop)
                    picked = jnp.where(match, part[k, b], picked)
            turned[b] = picked
        at = pl.ds(i * piece, piece)
        copies.append(pltpu.make_async_copy(turned.at[at], out.at[at], sems.at[i]))
        copies[-1].start()
    for copy in copies:
        copy.wait()


def turn_rest_kernel(first, bl, ln, plan, own, sibling, centroids, points_hbm, _, out, block):
    blocks, rows, _ = points_hbm.shape
    me = lax.axis_index("narrow")
    core = lax.rem(me, CORES)
    row_ids = lax.broadcasted_iota(i32, block.shape, 0) + me * rows

    @pl.loop(MOVE, blocks)
    def _(b):
        @pl.when(plan[b] >= first)
        def _():
            pltpu.sync_copy(points_hbm.at[b], block)
            kept = row_ids < ln[b]
            residual = jnp.where(kept, block[...].astype(f32) - centroids[pl.ds(bl[b], 1), :], 0.0).astype(bf16)
            at = lax.div(plan[b] - first, CORES)
            mine = lax.rem(plan[b], CORES) == core
            rotation = jnp.where(mine, own[at], sibling[at])
            block[...] = jnp.dot(residual, rotation, preferred_element_type=f32).astype(bf16)
            pltpu.sync_copy(block, out.at[b])


def local(wide, narrow, points, targets, centroids, block_list, lengths, sources):
    blocks, rows, width = points.shape
    lists = centroids.shape[0]
    per = lists // CORES
    chips = narrow // CORES
    mat = (width, width)
    lead = MOVE // CORES
    cap = per * 3 // 4 if chips == 2 else per
    rest = per - cap

    entries = blocks + 2 + MOVE
    table, residual, same, acc, send = call(
        gram_kernel,
        "grams",
        (
            jax.ShapeDtypeStruct((8, -(-entries // 128) * 128), i32),
            jax.ShapeDtypeStruct(points.shape, bf16),
            jax.ShapeDtypeStruct((MOVE, 8, width), f32),
            jax.ShapeDtypeStruct((lists,) + mat, f32),
            jax.ShapeDtypeStruct((lead,) + mat, bf16),
        ),
        [HBM] * 6,
        (VMEM,) * 5,
        tuple(stay(x) for x in (block_list, lengths, sources, points, targets, centroids)),
        scratch=[
            pltpu.SMEM((blocks,), i32),
            pltpu.SMEM((blocks,), i32),
            pltpu.SMEM((blocks,), i32),
            pltpu.SMEM((lists,), i32),
            pltpu.SMEM((entries,), i32),
            pltpu.VMEM(points.shape, bf16),
            pltpu.VMEM(points.shape, bf16),
            pltpu.VMEM(centroids.shape, f32),
            pltpu.SemaphoreType.DMA((2, PIECES)),
            pltpu.SemaphoreType.DMA((4,)),
        ],
    )

    to_core = [(i, i ^ 1) for i in range(narrow)]
    to_chip = [[(i, (i + CORES * k) % narrow) for i in range(narrow)] for k in range(1, chips)]

    def cross(part):
        return tuple(lax.ppermute(part, "narrow", perm) for perm in to_chip)

    def swap(part):
        return lax.ppermute(part, "narrow", to_core)

    recv = swap(send)
    counts = (lead, cap - lead) + (rest,) * (rest > 0)
    lead_chip, *sends = call(
        functools.partial(lead_sum_kernel, per),
        "lead_sum",
        tuple(jax.ShapeDtypeStruct((count,) + mat, bf16) for count in counts),
        [VMEM, VMEM],
        (VMEM,) * len(counts),
        (acc, recv),
    )
    lead_crossed = cross(lead_chip)
    recv_main = swap(sends[0])
    after = ()
    if rest:
        late_table = call(
            table_kernel,
            "table",
            jax.ShapeDtypeStruct(table.shape, i32),
            [VMEM, ANY],
            VMEM,
            (table, recv_main),
        )
        overflow = late_table[0, entries - 1] > CORES * cap
        after = (overflow.astype(i32).reshape(1),)
    main_chip = call(
        functools.partial(sum_kernel, lead),
        "main_sum",
        jax.ShapeDtypeStruct((cap - lead,) + mat, bf16),
        [VMEM, VMEM] + [ANY] * len(after),
        VMEM,
        (acc, recv_main, *after),
    )
    main_crossed = cross(main_chip)
    owns = [newton(acc, 0, lead, recv, 0, (lead_crossed,), (main_chip,))]
    siblings = [swap(owns[0])]

    leading = call(
        leading_kernel,
        "turn_leading",
        jax.ShapeDtypeStruct((MOVE, rows, width), bf16),
        [VMEM] * 4,
        VMEM,
        (same, residual, owns[0], siblings[0]),
        flops=LEAD_FLOPS,
    )
    starts, tokens = [0], ()
    if rest:
        starts.append(cap)
        rest_own, rest_chip = newton(acc, cap, rest, swap(sends[1]), 0, (), (leading,), True, 1 << 12)
        owns.append(rest_own)
        tokens = (rest_own,)
    if wide <= 16 and wide & (wide - 1) == 0:
        half = wide // 2
        far = lax.ppermute(leading, "wide", [(i, i ^ half) for i in range(wide)])
        pair = call(
            pair_kernel,
            "pair",
            jax.ShapeDtypeStruct((2,) + leading.shape, bf16),
            [VMEM, VMEM] + [ANY] * len(tokens),
            VMEM,
            (leading, far, *tokens),
            flops=PAIR_FLOPS,
        )
        order = range(half - 1, 0, -1)
        parts = [pair] + [lax.ppermute(pair, "wide", [(i, i ^ k) for i in range(wide)]) for k in order]
        hops = [(k, k ^ half) for k in [0, *order]]
        token = pair
    else:
        parts = [lax.all_gather(leading, "wide", axis=0)]
        hops = [tuple(range(wide))]
        token = leading
    main = newton(acc, lead, cap - lead, recv_main, 0, (main_crossed,), (token,))
    siblings += [swap(own) for own in owns[1:]]
    other = swap(main)

    rots = call(
        functools.partial(gather_kernel, starts + [lead], len(owns) + 1),
        "gather_rotations",
        jax.ShapeDtypeStruct((lists,) + mat, bf16),
        [VMEM] * (1 + len(owns) + len(siblings)),
        VMEM,
        (*owns, main, *siblings),
    )
    token = call(
        arrived_kernel,
        "arrived",
        jax.ShapeDtypeStruct((8, 128), f32),
        [ANY] * (1 + len(parts)),
        VMEM,
        (*parts, rots),
        moved=LONG,
    )
    turned, _ = call(
        functools.partial(turn_kernel, lead, hops),
        "turn",
        (pltpu.HBM(points.shape, bf16), jax.ShapeDtypeStruct(rots.shape, bf16)),
        [VMEM] * (4 + len(parts)) + [ANY],
        (HBM, VMEM),
        (table, residual, other, rots, *parts, token),
        scratch=[
            pltpu.VMEM(points.shape, bf16),
            pltpu.SemaphoreType.DMA((STORES,)),
        ],
        aliases={3: 1},
    )
    if not rest:
        return turned

    def exchange_rest(state):
        turned, chip = state
        own = call(
            functools.partial(newton_rest_kernel, len(to_chip)),
            "newton_rest",
            jax.ShapeDtypeStruct(chip.shape, bf16),
            [VMEM] * (1 + len(to_chip)),
            VMEM,
            (chip, *cross(chip.astype(bf16))),
        )
        turned = call(
            functools.partial(turn_rest_kernel, CORES * cap),
            "turn_rest",
            pltpu.HBM(turned.shape, bf16),
            [SMEM] * 3 + [VMEM] * 3 + [HBM] * 2,
            HBM,
            (block_list, lengths, table[0, :blocks], own, swap(own), centroids, stay(points), stay(turned)),
            scratch=[pltpu.VMEM((rows, width), bf16)],
            aliases={7: 0},
        )
        return turned

    return lax.cond(overflow, exchange_rest, lambda state: state[0], (turned, rest_chip))


def solution(mesh):
    return jax.shard_map(
        functools.partial(local, mesh.shape["wide"], mesh.shape["narrow"]),
        mesh=mesh,
        in_specs=(
            P("wide", "narrow", None),
            P("wide", "narrow", None),
            P("wide", None),
            P("wide"),
            P("wide"),
            P("wide"),
        ),
        out_specs=P("wide", "narrow", None),
        check_vma=False,
    )
```

```python
import functools

import jax
import jax.numpy as jnp
from jax import lax
from jax.experimental import pallas as pl
from jax.experimental.pallas import tpu as pltpu
from jax.sharding import PartitionSpec as P

MOVE = 2
ITERS = 5
CORES = 2
PIECES = 2
STORES = 8
VMEM_LIMIT = 14 * 1024 * 1024
LONG = 1 << 30
GROUP = 4
LEAD_FLOPS = 1350000000
PAIR_FLOPS = 1500000000

f32, bf16, i32 = jnp.float32, jnp.bfloat16, jnp.int32

SMEM = pl.BlockSpec(memory_space=pltpu.SMEM)
VMEM = pl.BlockSpec(memory_space=pltpu.VMEM)
HBM = pl.BlockSpec(memory_space=pltpu.HBM)
ANY = pl.BlockSpec(memory_space=pl.ANY)


def stay(x):
    return pltpu.with_memory_space_constraint(x, pltpu.HBM)


def call(kernel, name, outs, in_specs, out_specs, args, moved=1 << 20, flops=0, scratch=(), aliases={}):
    return pl.pallas_call(
        kernel,
        out_shape=outs,
        in_specs=in_specs,
        out_specs=out_specs,
        scratch_shapes=scratch,
        input_output_aliases=aliases,
        compiler_params=pltpu.CompilerParams(vmem_limit_bytes=VMEM_LIMIT),
        cost_estimate=pl.CostEstimate(flops=16 * moved if moved == LONG else flops, bytes_accessed=moved, transcendentals=0),
        name=name,
    )(*args)


def assign_slots(bl, ln, first_rows, slot_of_list, plan):
    blocks, lists = bl.shape[0], slot_of_list.shape[0]
    for l in range(lists):
        slot_of_list[l] = -1

    def visit(b, nxt, wanted):
        l = bl[b]
        s = slot_of_list[l]
        new = jnp.logical_and(s < 0, wanted)
        slot_of_list[l] = jnp.where(new, nxt, s)
        return nxt + new.astype(i32)

    nxt = jnp.int32(0)
    for b in range(MOVE):
        nxt = visit(b, nxt, True)
    for b in range(MOVE, blocks):
        nxt = visit(b, nxt, ln[b] > first_rows)
    plan[blocks + 1 + MOVE] = nxt
    for b in range(MOVE, blocks):
        nxt = visit(b, nxt, True)
    plan[blocks] = nxt
    for b in range(blocks):
        plan[b] = slot_of_list[bl[b]]


def gram_kernel(bl_hbm, ln_hbm, sources_hbm, points_hbm, targets_hbm, centroids_hbm, table, residual, same, acc, send, *scratch):
    bl, ln, sources, slot_of_list, plan, points, targets, centroids, sems, int_sems = scratch
    blocks, rows, _ = points.shape
    per = acc.shape[0] // CORES
    piece = blocks // PIECES
    copies = [
        pltpu.make_async_copy(bl_hbm, bl, int_sems.at[0]),
        pltpu.make_async_copy(ln_hbm, ln, int_sems.at[1]),
        pltpu.make_async_copy(centroids_hbm, centroids, int_sems.at[2]),
        pltpu.make_async_copy(sources_hbm, sources, int_sems.at[3]),
    ]
    for copy in copies:
        copy.start()
    parts = []
    for i in range(PIECES):
        at = pl.ds(i * piece, piece)
        pair = (
            pltpu.make_async_copy(points_hbm.at[at], points.at[at], sems.at[0, i]),
            pltpu.make_async_copy(targets_hbm.at[at], targets.at[at], sems.at[1, i]),
        )
        for copy in pair:
            copy.start()
        parts.append(pair)
    me = lax.axis_index("narrow")
    core = lax.rem(me, CORES)
    acc[...] = jnp.zeros_like(acc)
    copies[0].wait()
    copies[1].wait()
    assign_slots(bl, ln, CORES * rows, slot_of_list, plan)
    copies[2].wait()
    copies[3].wait()
    for j in range(MOVE):
        plan[blocks + 1 + j] = lax.div(sources[j], blocks)
        mine = lax.rem(plan[j], CORES) == core
        same[j] = jnp.full(same.shape[1:], jnp.where(mine, 1.0, 0.0), f32)
    lanes = lax.broadcasted_iota(i32, table.shape, 1)
    entries = jnp.zeros(table.shape, i32)
    for k in range(plan.shape[0]):
        entries = jnp.where(lanes == k, plan[k], entries)
    table[...] = entries
    row_ids = lax.broadcasted_iota(i32, points.shape[1:], 0) + me * rows
    for i in range(PIECES):
        for copy in parts[i]:
            copy.wait()
        for b in range(i * piece, (i + 1) * piece):
            kept = row_ids < ln[b]
            res = jnp.where(kept, points[b].astype(f32) - centroids[pl.ds(bl[b], 1), :], 0.0).astype(bf16)
            residual[b] = res
            slot = plan[b]
            at = lax.div(slot, CORES) + jnp.where(lax.rem(slot, CORES) == core, 0, per)
            acc[at] += lax.dot_general(res, targets[b], (((0,), (0,)), ((), ())), preferred_element_type=f32)
    for i in range(send.shape[0]):
        send[i] = acc[per + i].astype(bf16)


def lead_sum_kernel(per, acc, recv, chip, *sends):
    at = chip.shape[0]
    chip[...] = (acc[:at] + recv[...].astype(f32)).astype(bf16)
    for out in sends:
        count = out.shape[0]
        out[...] = acc[per + at:per + at + count].astype(bf16)
        at += count


def table_kernel(table, _, out):
    out[...] = table[...]


def sum_kernel(first, acc, recv, *refs):
    out = refs[-1]
    count = out.shape[0]
    out[...] = (acc[first:first + count] + recv[...].astype(f32)).astype(bf16)


def newton_kernel(count, first, offset, extra, keep, acc, recv, *refs):
    pieces, out, chip = refs[:-2], refs[-2], refs[-1]
    grams = []
    for i in range(count):
        g = acc[first + i] + recv[offset + i].astype(f32)
        if keep:
            chip[i] = g
        for which in extra:
            piece, row = which[i]
            g = g + pieces[piece][row].astype(f32)
        grams.append(g)
    polar(grams, out)


def polar(grams, out):
    xs = []
    for g in grams:
        gb = g.astype(bf16)
        p = lax.dot_general(gb, gb, (((1,), (1,)), ((), ())), preferred_element_type=f32)
        scale = lax.rsqrt(jnp.sum(g * g) + 1e-6)
        p = (p * (scale * scale)).astype(bf16)
        xs.append((1.5 * scale) * g - (0.5 * scale) * jnp.dot(p, gb, preferred_element_type=f32))
    for _ in range(ITERS - 1):
        for i, x in enumerate(xs):
            xb = x.astype(bf16)
            p = lax.dot_general(xb, xb, (((1,), (1,)), ((), ())), preferred_element_type=f32).astype(bf16)
            xs[i] = 1.5 * x - 0.5 * jnp.dot(p, xb, preferred_element_type=f32)
    for i, x in enumerate(xs):
        out[i] = x.astype(bf16)


def newton(acc, first, count, recv, offset, crossed, after=(), keep=False, moved=1 << 20):
    extra = [[] for _ in (crossed[0] if crossed else ())]
    flat = []
    for group in crossed:
        for chip, part in enumerate(group):
            extra[chip] += [(len(flat), row) for row in range(part.shape[0])]
            flat.append(part)
    shape = (count,) + acc.shape[1:]
    out = call(
        functools.partial(newton_kernel, count, first, offset, extra, keep),
        "newton",
        (jax.ShapeDtypeStruct(shape, bf16),) + ((jax.ShapeDtypeStruct(shape, f32),) if keep else ()),
        [VMEM] * (2 + len(flat)) + [ANY] * len(after),
        (VMEM,) * (1 + keep),
        (acc, recv, *flat, *after),
        moved=moved,
        scratch=[] if keep else [pltpu.VMEM((8, 128), f32)],
    )
    return out if keep else out[0]


def newton_rest_kernel(others, chip, *refs):
    out = refs[-1]
    grams = []
    for i in range(chip.shape[0]):
        g = chip[i]
        for other in refs[:others]:
            g = g + other[i].astype(f32)
        grams.append(g)
    polar(grams, out)


def leading_kernel(same, residual, own, sibling, out):
    for b in range(MOVE):
        rotation = jnp.where(same[b, :1] > 0.5, own[0], sibling[0])
        out[b] = jnp.dot(residual[b], rotation, preferred_element_type=f32).astype(bf16)


def pair_kernel(near, far, *refs):
    out = refs[-1]
    out[0] = near[...]
    out[1] = far[...]


def arrived_kernel(*refs):
    refs[-1][...] = jnp.zeros_like(refs[-1])


def gather_kernel(starts, n_own, *refs):
    owns, siblings, rots = refs[:n_own], refs[n_own:-1], refs[-1]
    core = lax.rem(lax.axis_index("narrow"), CORES)
    for s, own in zip(starts, owns):
        for i in range(own.shape[0]):
            rots[CORES * (s + i) + core] = own[i]
    for s, sibling in zip(starts, siblings):
        for i in range(sibling.shape[0]):
            rots[CORES * (s + i) + 1 - core] = sibling[i]


def turn_kernel(first, hops, table, residual, main, _, *refs):
    parts = refs[:len(hops)]
    out, rots, turned, sems = refs[-4:]
    blocks, rows, _ = residual.shape
    piece = blocks // STORES
    core = lax.rem(lax.axis_index("narrow"), CORES)
    here = lax.axis_index("wide")
    plan = table[...]
    for i in range(main.shape[0]):
        rots[CORES * (first + i) + 1 - core] = main[i]
    copies = []
    for i in reversed(range(STORES)):
        for b in reversed(range(i * piece, (i + 1) * piece)):
            if b >= MOVE:
                turned[b] = jnp.dot(residual[b], rots[plan[0, b]], preferred_element_type=f32).astype(bf16)
                continue
            donor = plan[0, blocks + 1 + b]
            picked = parts[0][0, b]
            for part, group in zip(parts, hops):
                for k, hop in enumerate(group):
                    match = donor == (hop if len(parts) == 1 else here ^ hop)
                    picked = jnp.where(match, part[k, b], picked)
            turned[b] = picked
        at = pl.ds(i * piece, piece)
        copies.append(pltpu.make_async_copy(turned.at[at], out.at[at], sems.at[i]))
        copies[-1].start()
    for copy in copies:
        copy.wait()


def turn_rest_kernel(first, last, bl, ln, plan, own, sibling, centroids, points_hbm, _, out, block):
    blocks, rows, _ = points_hbm.shape
    me = lax.axis_index("narrow")
    core = lax.rem(me, CORES)
    row_ids = lax.broadcasted_iota(i32, block.shape, 0) + me * rows

    @pl.loop(MOVE, blocks)
    def _(b):
        @pl.when(jnp.logical_and(plan[b] >= first, plan[b] < plan[last]))
        def _():
            pltpu.sync_copy(points_hbm.at[b], block)
            kept = row_ids < ln[b]
            residual = jnp.where(kept, block[...].astype(f32) - centroids[pl.ds(bl[b], 1), :], 0.0).astype(bf16)
            at = lax.div(plan[b] - first, CORES)
            mine = lax.rem(plan[b], CORES) == core
            rotation = jnp.where(mine, own[at], sibling[at])
            block[...] = jnp.dot(residual, rotation, preferred_element_type=f32).astype(bf16)
            pltpu.sync_copy(block, out.at[b])


def local(wide, narrow, points, targets, centroids, block_list, lengths, sources):
    blocks, rows, width = points.shape
    lists = centroids.shape[0]
    per = lists // CORES
    chips = narrow // CORES
    mat = (width, width)
    lead = MOVE // CORES
    cap = per * 3 // 4 if chips == 2 else per
    rest = per - cap

    entries = blocks + 2 + MOVE
    table, residual, same, acc, send = call(
        gram_kernel,
        "grams",
        (
            jax.ShapeDtypeStruct((8, -(-entries // 128) * 128), i32),
            jax.ShapeDtypeStruct(points.shape, bf16),
            jax.ShapeDtypeStruct((MOVE, 8, width), f32),
            jax.ShapeDtypeStruct((lists,) + mat, f32),
            jax.ShapeDtypeStruct((lead,) + mat, bf16),
        ),
        [HBM] * 6,
        (VMEM,) * 5,
        tuple(stay(x) for x in (block_list, lengths, sources, points, targets, centroids)),
        scratch=[
            pltpu.SMEM((blocks,), i32),
            pltpu.SMEM((blocks,), i32),
            pltpu.SMEM((blocks,), i32),
            pltpu.SMEM((lists,), i32),
            pltpu.SMEM((entries,), i32),
            pltpu.VMEM(points.shape, bf16),
            pltpu.VMEM(points.shape, bf16),
            pltpu.VMEM(centroids.shape, f32),
            pltpu.SemaphoreType.DMA((2, PIECES)),
            pltpu.SemaphoreType.DMA((4,)),
        ],
    )

    to_core = [(i, i ^ 1) for i in range(narrow)]
    to_chip = [[(i, (i + CORES * k) % narrow) for i in range(narrow)] for k in range(1, chips)]

    def cross(part):
        return tuple(lax.ppermute(part, "narrow", perm) for perm in to_chip)

    def swap(part):
        return lax.ppermute(part, "narrow", to_core)

    recv = swap(send)
    counts = (lead, cap - lead) + (rest,) * (rest > 0)
    lead_chip, *sends = call(
        functools.partial(lead_sum_kernel, per),
        "lead_sum",
        tuple(jax.ShapeDtypeStruct((count,) + mat, bf16) for count in counts),
        [VMEM, VMEM],
        (VMEM,) * len(counts),
        (acc, recv),
    )
    lead_crossed = cross(lead_chip)
    recv_main = swap(sends[0])
    after = ()
    if rest:
        late_table = call(
            table_kernel,
            "table",
            jax.ShapeDtypeStruct(table.shape, i32),
            [VMEM, ANY],
            VMEM,
            (table, recv_main),
        )
        overflow = late_table[0, entries - 1] > CORES * cap
        after = (overflow.astype(i32).reshape(1),)
    main_chip = call(
        functools.partial(sum_kernel, lead),
        "main_sum",
        jax.ShapeDtypeStruct((cap - lead,) + mat, bf16),
        [VMEM, VMEM] + [ANY] * len(after),
        VMEM,
        (acc, recv_main, *after),
    )
    main_crossed = cross(main_chip)
    owns = [newton(acc, 0, lead, recv, 0, (lead_crossed,), (main_chip,))]
    siblings = [swap(owns[0])]

    leading = call(
        leading_kernel,
        "turn_leading",
        jax.ShapeDtypeStruct((MOVE, rows, width), bf16),
        [VMEM] * 4,
        VMEM,
        (same, residual, owns[0], siblings[0]),
        flops=LEAD_FLOPS,
    )
    starts, tokens = [0], ()
    if rest:
        starts.append(cap)
        rest_own, rest_chip = newton(acc, cap, rest, swap(sends[1]), 0, (), (leading,), True, 1 << 12)
        owns.append(rest_own)
        tokens = (rest_own,)
    if wide <= 16 and wide & (wide - 1) == 0:
        half = wide // 2
        far = lax.ppermute(leading, "wide", [(i, i ^ half) for i in range(wide)])
        pair = call(
            pair_kernel,
            "pair",
            jax.ShapeDtypeStruct((2,) + leading.shape, bf16),
            [VMEM, VMEM] + [ANY] * len(tokens),
            VMEM,
            (leading, far, *tokens),
            flops=PAIR_FLOPS,
        )
        order = range(half - 1, 0, -1)
        parts = [pair] + [lax.ppermute(pair, "wide", [(i, i ^ k) for i in range(wide)]) for k in order]
        hops = [(k, k ^ half) for k in [0, *order]]
        token = pair
    else:
        parts = [lax.all_gather(leading, "wide", axis=0)]
        hops = [tuple(range(wide))]
        token = leading
    main = newton(acc, lead, cap - lead, recv_main, 0, (main_crossed,), (token,))
    siblings += [swap(own) for own in owns[1:]]
    other = swap(main)

    rots = call(
        functools.partial(gather_kernel, starts + [lead], len(owns) + 1),
        "gather_rotations",
        jax.ShapeDtypeStruct((lists,) + mat, bf16),
        [VMEM] * (1 + len(owns) + len(siblings)),
        VMEM,
        (*owns, main, *siblings),
    )
    token = call(
        arrived_kernel,
        "arrived",
        jax.ShapeDtypeStruct((8, 128), f32),
        [ANY] * (1 + len(parts)),
        VMEM,
        (*parts, rots),
        moved=LONG,
    )
    turned, _ = call(
        functools.partial(turn_kernel, lead, hops),
        "turn",
        (pltpu.HBM(points.shape, bf16), jax.ShapeDtypeStruct(rots.shape, bf16)),
        [VMEM] * (4 + len(parts)) + [ANY],
        (HBM, VMEM),
        (table, residual, other, rots, *parts, token),
        scratch=[
            pltpu.VMEM(points.shape, bf16),
            pltpu.SemaphoreType.DMA((STORES,)),
        ],
        aliases={3: 1},
    )
    if not rest:
        return turned

    def exchange_rest(state):
        turned, chip = state
        own = call(
            functools.partial(newton_rest_kernel, len(to_chip)),
            "newton_rest",
            jax.ShapeDtypeStruct(chip.shape, bf16),
            [VMEM] * (1 + len(to_chip)),
            VMEM,
            (chip, *cross(chip.astype(bf16))),
        )
        turned = call(
            functools.partial(turn_rest_kernel, CORES * cap, entries - 1),
            "turn_rest",
            pltpu.HBM(turned.shape, bf16),
            [SMEM] * 3 + [VMEM] * 3 + [HBM] * 2,
            HBM,
            (block_list, lengths, table[0, :entries], own, swap(own), centroids, stay(points), stay(turned)),
            scratch=[pltpu.VMEM((rows, width), bf16)],
            aliases={7: 0},
        )
        return turned

    return lax.cond(overflow, exchange_rest, lambda state: state[0], (turned, rest_chip))


def solution(mesh):
    return jax.shard_map(
        functools.partial(local, mesh.shape["wide"], mesh.shape["narrow"]),
        mesh=mesh,
        in_specs=(
            P("wide", "narrow", None),
            P("wide", "narrow", None),
            P("wide", None),
            P("wide"),
            P("wide"),
            P("wide"),
        ),
        out_specs=P("wide", "narrow", None),
        check_vma=False,
    )
```

```python
import functools

import jax
import jax.numpy as jnp
from jax import lax
from jax.experimental import pallas as pl
from jax.experimental.pallas import tpu as pltpu
from jax.sharding import PartitionSpec as P

MOVE = 2
ITERS = 5
CORES = 2
PIECES = 2
STORES = 8
VMEM_LIMIT = 14 * 1024 * 1024
LONG = 1 << 30
GROUP = 4
LEAD_FLOPS = 1350000000
PAIR_FLOPS = 1500000000

f32, bf16, i32 = jnp.float32, jnp.bfloat16, jnp.int32

SMEM = pl.BlockSpec(memory_space=pltpu.SMEM)
VMEM = pl.BlockSpec(memory_space=pltpu.VMEM)
HBM = pl.BlockSpec(memory_space=pltpu.HBM)
ANY = pl.BlockSpec(memory_space=pl.ANY)


def stay(x):
    return pltpu.with_memory_space_constraint(x, pltpu.HBM)


def call(kernel, name, outs, in_specs, out_specs, args, moved=1 << 20, flops=0, scratch=(), aliases={}):
    return pl.pallas_call(
        kernel,
        out_shape=outs,
        in_specs=in_specs,
        out_specs=out_specs,
        scratch_shapes=scratch,
        input_output_aliases=aliases,
        compiler_params=pltpu.CompilerParams(vmem_limit_bytes=VMEM_LIMIT),
        cost_estimate=pl.CostEstimate(flops=16 * moved if moved == LONG else flops, bytes_accessed=moved, transcendentals=0),
        name=name,
    )(*args)


def assign_slots(bl, ln, first_rows, slot_of_list, plan):
    blocks, lists = bl.shape[0], slot_of_list.shape[0]
    for l in range(lists):
        slot_of_list[l] = -1

    def visit(b, nxt, wanted):
        l = bl[b]
        s = slot_of_list[l]
        new = jnp.logical_and(s < 0, wanted)
        slot_of_list[l] = jnp.where(new, nxt, s)
        return nxt + new.astype(i32)

    nxt = jnp.int32(0)
    for b in range(MOVE):
        nxt = visit(b, nxt, True)
    for b in range(MOVE, blocks):
        nxt = visit(b, nxt, ln[b] > first_rows)
    plan[blocks + 1 + MOVE] = nxt
    for b in range(MOVE, blocks):
        nxt = visit(b, nxt, True)
    plan[blocks] = nxt
    for b in range(blocks):
        plan[b] = slot_of_list[bl[b]]


def gram_kernel(bl_hbm, ln_hbm, sources_hbm, points_hbm, targets_hbm, centroids_hbm, table, residual, same, acc, send, *scratch):
    bl, ln, sources, slot_of_list, plan, points, targets, centroids, sems, int_sems = scratch
    blocks, rows, _ = points.shape
    per = acc.shape[0] // CORES
    piece = blocks // PIECES
    copies = [
        pltpu.make_async_copy(bl_hbm, bl, int_sems.at[0]),
        pltpu.make_async_copy(ln_hbm, ln, int_sems.at[1]),
        pltpu.make_async_copy(centroids_hbm, centroids, int_sems.at[2]),
        pltpu.make_async_copy(sources_hbm, sources, int_sems.at[3]),
    ]
    for copy in copies:
        copy.start()
    parts = []
    for i in range(PIECES):
        at = pl.ds(i * piece, piece)
        pair = (
            pltpu.make_async_copy(points_hbm.at[at], points.at[at], sems.at[0, i]),
            pltpu.make_async_copy(targets_hbm.at[at], targets.at[at], sems.at[1, i]),
        )
        for copy in pair:
            copy.start()
        parts.append(pair)
    me = lax.axis_index("narrow")
    core = lax.rem(me, CORES)
    acc[...] = jnp.zeros_like(acc)
    copies[0].wait()
    copies[1].wait()
    assign_slots(bl, ln, CORES * rows, slot_of_list, plan)
    copies[2].wait()
    copies[3].wait()
    for j in range(MOVE):
        plan[blocks + 1 + j] = lax.div(sources[j], blocks)
        mine = lax.rem(plan[j], CORES) == core
        same[j] = jnp.full(same.shape[1:], jnp.where(mine, 1.0, 0.0), f32)
    lanes = lax.broadcasted_iota(i32, table.shape, 1)
    entries = jnp.zeros(table.shape, i32)
    for k in range(plan.shape[0]):
        entries = jnp.where(lanes == k, plan[k], entries)
    table[...] = entries
    row_ids = lax.broadcasted_iota(i32, points.shape[1:], 0) + me * rows
    for i in range(PIECES):
        for copy in parts[i]:
            copy.wait()
        for b in range(i * piece, (i + 1) * piece):
            kept = row_ids < ln[b]
            res = jnp.where(kept, points[b].astype(f32) - centroids[pl.ds(bl[b], 1), :], 0.0).astype(bf16)
            residual[b] = res
            slot = plan[b]
            at = lax.div(slot, CORES) + jnp.where(lax.rem(slot, CORES) == core, 0, per)
            acc[at] += lax.dot_general(res, targets[b], (((0,), (0,)), ((), ())), preferred_element_type=f32)
    for i in range(send.shape[0]):
        send[i] = acc[per + i].astype(bf16)


def lead_sum_kernel(per, acc, recv, chip, *sends):
    at = chip.shape[0]
    chip[...] = (acc[:at] + recv[...].astype(f32)).astype(bf16)
    for out in sends:
        count = out.shape[0]
        out[...] = acc[per + at:per + at + count].astype(bf16)
        at += count


def table_kernel(table, _, out):
    out[...] = table[...]


def sum_kernel(first, acc, recv, *refs):
    out = refs[-1]
    count = out.shape[0]
    out[...] = (acc[first:first + count] + recv[...].astype(f32)).astype(bf16)


def newton_kernel(count, first, offset, extra, keep, acc, recv, *refs):
    pieces, out, chip = refs[:-2], refs[-2], refs[-1]
    grams = []
    for i in range(count):
        g = acc[first + i] + recv[offset + i].astype(f32)
        if keep:
            chip[i] = g
        for which in extra:
            piece, row = which[i]
            g = g + pieces[piece][row].astype(f32)
        grams.append(g)
    polar(grams, out)


def polar(grams, out):
    xs = []
    for g in grams:
        gb = g.astype(bf16)
        p = lax.dot_general(gb, gb, (((1,), (1,)), ((), ())), preferred_element_type=f32)
        scale = lax.rsqrt(jnp.sum(g * g) + 1e-6)
        p = (p * (scale * scale)).astype(bf16)
        xs.append((1.5 * scale) * g - (0.5 * scale) * jnp.dot(p, gb, preferred_element_type=f32))
    for _ in range(ITERS - 1):
        for i, x in enumerate(xs):
            xb = x.astype(bf16)
            p = lax.dot_general(xb, xb, (((1,), (1,)), ((), ())), preferred_element_type=f32).astype(bf16)
            xs[i] = 1.5 * x - 0.5 * jnp.dot(p, xb, preferred_element_type=f32)
    for i, x in enumerate(xs):
        out[i] = x.astype(bf16)


def newton(acc, first, count, recv, offset, crossed, after=(), keep=False, moved=1 << 20):
    extra = [[] for _ in (crossed[0] if crossed else ())]
    flat = []
    for group in crossed:
        for chip, part in enumerate(group):
            extra[chip] += [(len(flat), row) for row in range(part.shape[0])]
            flat.append(part)
    shape = (count,) + acc.shape[1:]
    out = call(
        functools.partial(newton_kernel, count, first, offset, extra, keep),
        "newton",
        (jax.ShapeDtypeStruct(shape, bf16),) + ((jax.ShapeDtypeStruct(shape, f32),) if keep else ()),
        [VMEM] * (2 + len(flat)) + [ANY] * len(after),
        (VMEM,) * (1 + keep),
        (acc, recv, *flat, *after),
        moved=moved,
        scratch=[] if keep else [pltpu.VMEM((8, 128), f32)],
    )
    return out if keep else out[0]


def newton_rest_kernel(others, chip, *refs):
    out = refs[-1]
    grams = []
    for i in range(chip.shape[0]):
        g = chip[i]
        for other in refs[:others]:
            g = g + other[i].astype(f32)
        grams.append(g)
    polar(grams, out)


def leading_kernel(same, residual, own, sibling, out):
    for b in range(MOVE):
        rotation = jnp.where(same[b, :1] > 0.5, own[0], sibling[0])
        out[b] = jnp.dot(residual[b], rotation, preferred_element_type=f32).astype(bf16)


def pair_kernel(near, far, *refs):
    out = refs[-1]
    out[0] = near[...]
    out[1] = far[...]


def arrived_kernel(*refs):
    refs[-1][...] = jnp.zeros_like(refs[-1])


def gather_kernel(starts, n_own, *refs):
    owns, siblings, rots = refs[:n_own], refs[n_own:-1], refs[-1]
    core = lax.rem(lax.axis_index("narrow"), CORES)
    for s, own in zip(starts, owns):
        for i in range(own.shape[0]):
            rots[CORES * (s + i) + core] = own[i]
    for s, sibling in zip(starts, siblings):
        for i in range(sibling.shape[0]):
            rots[CORES * (s + i) + 1 - core] = sibling[i]


def turn_kernel(first, hops, table, residual, main, _, *refs):
    parts = refs[:len(hops)]
    out, rots, turned, sems = refs[-4:]
    blocks, rows, _ = residual.shape
    piece = blocks // STORES
    core = lax.rem(lax.axis_index("narrow"), CORES)
    here = lax.axis_index("wide")
    plan = table[...]
    for i in range(main.shape[0]):
        rots[CORES * (first + i) + 1 - core] = main[i]
    copies = []
    for i in reversed(range(STORES)):
        for b in reversed(range(i * piece, (i + 1) * piece)):
            if b >= MOVE:
                turned[b] = jnp.dot(residual[b], rots[plan[0, b]], preferred_element_type=f32).astype(bf16)
                continue
            donor = plan[0, blocks + 1 + b]
            picked = parts[0][0, b]
            for part, group in zip(parts, hops):
                for k, hop in enumerate(group):
                    match = donor == (hop if len(parts) == 1 else here ^ hop)
                    picked = jnp.where(match, part[k, b], picked)
            turned[b] = picked
        at = pl.ds(i * piece, piece)
        copies.append(pltpu.make_async_copy(turned.at[at], out.at[at], sems.at[i]))
        copies[-1].start()
    for copy in copies:
        copy.wait()


def turn_rest_kernel(first, last, bl, ln, plan, own, sibling, centroids, points_hbm, _, out, block):
    blocks, rows, _ = points_hbm.shape
    me = lax.axis_index("narrow")
    core = lax.rem(me, CORES)
    row_ids = lax.broadcasted_iota(i32, block.shape, 0) + me * rows

    @pl.loop(MOVE, blocks)
    def _(b):
        @pl.when(jnp.logical_and(plan[b] >= first, plan[b] < plan[last]))
        def _():
            pltpu.sync_copy(points_hbm.at[b], block)
            kept = row_ids < ln[b]
            residual = jnp.where(kept, block[...].astype(f32) - centroids[pl.ds(bl[b], 1), :], 0.0).astype(bf16)
            at = lax.div(plan[b] - first, CORES)
            mine = lax.rem(plan[b], CORES) == core
            rotation = jnp.where(mine, own[at], sibling[at])
            block[...] = jnp.dot(residual, rotation, preferred_element_type=f32).astype(bf16)
            pltpu.sync_copy(block, out.at[b])


def local(wide, narrow, points, targets, centroids, block_list, lengths, sources):
    blocks, rows, width = points.shape
    lists = centroids.shape[0]
    per = lists // CORES
    chips = narrow // CORES
    mat = (width, width)
    lead = MOVE // CORES
    cap = per * 3 // 4 if chips == 2 else per
    rest = per - cap

    entries = blocks + 2 + MOVE
    table, residual, same, acc, send = call(
        gram_kernel,
        "grams",
        (
            jax.ShapeDtypeStruct((8, -(-entries // 128) * 128), i32),
            jax.ShapeDtypeStruct(points.shape, bf16),
            jax.ShapeDtypeStruct((MOVE, 8, width), f32),
            jax.ShapeDtypeStruct((lists,) + mat, f32),
            jax.ShapeDtypeStruct((lead,) + mat, bf16),
        ),
        [HBM] * 6,
        (VMEM,) * 5,
        tuple(stay(x) for x in (block_list, lengths, sources, points, targets, centroids)),
        scratch=[
            pltpu.SMEM((blocks,), i32),
            pltpu.SMEM((blocks,), i32),
            pltpu.SMEM((blocks,), i32),
            pltpu.SMEM((lists,), i32),
            pltpu.SMEM((entries,), i32),
            pltpu.VMEM(points.shape, bf16),
            pltpu.VMEM(points.shape, bf16),
            pltpu.VMEM(centroids.shape, f32),
            pltpu.SemaphoreType.DMA((2, PIECES)),
            pltpu.SemaphoreType.DMA((4,)),
        ],
    )

    to_core = [(i, i ^ 1) for i in range(narrow)]
    to_chip = [[(i, (i + CORES * k) % narrow) for i in range(narrow)] for k in range(1, chips)]

    def cross(part):
        return tuple(lax.ppermute(part, "narrow", perm) for perm in to_chip)

    def swap(part):
        return lax.ppermute(part, "narrow", to_core)

    recv = swap(send)
    counts = (lead, cap - lead) + (rest,) * (rest > 0)
    lead_chip, *sends = call(
        functools.partial(lead_sum_kernel, per),
        "lead_sum",
        tuple(jax.ShapeDtypeStruct((count,) + mat, bf16) for count in counts),
        [VMEM, VMEM],
        (VMEM,) * len(counts),
        (acc, recv),
    )
    lead_crossed = cross(lead_chip)
    recv_main = swap(sends[0])
    after = ()
    if rest:
        late_table = call(
            table_kernel,
            "table",
            jax.ShapeDtypeStruct(table.shape, i32),
            [VMEM, ANY],
            VMEM,
            (table, recv_main),
        )
        overflow = late_table[0, entries - 1] > CORES * cap
        after = (overflow.astype(i32).reshape(1),)
    main_chip = call(
        functools.partial(sum_kernel, lead),
        "main_sum",
        jax.ShapeDtypeStruct((cap - lead,) + mat, bf16),
        [VMEM, VMEM] + [ANY] * len(after),
        VMEM,
        (acc, recv_main, *after),
    )
    main_crossed = cross(main_chip)
    owns = [newton(acc, 0, lead, recv, 0, (lead_crossed,), (main_chip,))]
    siblings = [swap(owns[0])]

    leading = call(
        leading_kernel,
        "turn_leading",
        jax.ShapeDtypeStruct((MOVE, rows, width), bf16),
        [VMEM] * 4,
        VMEM,
        (same, residual, owns[0], siblings[0]),
        flops=LEAD_FLOPS,
    )
    starts, tokens = [0], ()
    if rest:
        starts.append(cap)
        rest_own, rest_chip = newton(acc, cap, rest, swap(sends[1]), 0, (), (leading,), True, 1 << 12)
        owns.append(rest_own)
        tokens = (rest_own,)
    if wide <= 16 and wide & (wide - 1) == 0:
        half = wide // 2
        far = lax.ppermute(leading, "wide", [(i, i ^ half) for i in range(wide)])
        pair = call(
            pair_kernel,
            "pair",
            jax.ShapeDtypeStruct((2,) + leading.shape, bf16),
            [VMEM, VMEM] + [ANY] * len(tokens),
            VMEM,
            (leading, far, *tokens),
            flops=PAIR_FLOPS,
        )
        order = (half - 1, *range(1, half - 1))
        parts = [pair] + [lax.ppermute(pair, "wide", [(i, i ^ k) for i in range(wide)]) for k in order]
        hops = [(k, k ^ half) for k in [0, *order]]
        token = pair
    else:
        parts = [lax.all_gather(leading, "wide", axis=0)]
        hops = [tuple(range(wide))]
        token = leading
    main = newton(acc, lead, cap - lead, recv_main, 0, (main_crossed,), (token,))
    siblings += [swap(own) for own in owns[1:]]
    other = swap(main)

    rots = call(
        functools.partial(gather_kernel, starts + [lead], len(owns) + 1),
        "gather_rotations",
        jax.ShapeDtypeStruct((lists,) + mat, bf16),
        [VMEM] * (1 + len(owns) + len(siblings)),
        VMEM,
        (*owns, main, *siblings),
    )
    token = call(
        arrived_kernel,
        "arrived",
        jax.ShapeDtypeStruct((8, 128), f32),
        [ANY] * (1 + len(parts)),
        VMEM,
        (*parts, rots),
        moved=LONG,
    )
    turned, _ = call(
        functools.partial(turn_kernel, lead, hops),
        "turn",
        (pltpu.HBM(points.shape, bf16), jax.ShapeDtypeStruct(rots.shape, bf16)),
        [VMEM] * (4 + len(parts)) + [ANY],
        (HBM, VMEM),
        (table, residual, other, rots, *parts, token),
        scratch=[
            pltpu.VMEM(points.shape, bf16),
            pltpu.SemaphoreType.DMA((STORES,)),
        ],
        aliases={3: 1},
    )
    if not rest:
        return turned

    def exchange_rest(state):
        turned, chip = state
        own = call(
            functools.partial(newton_rest_kernel, len(to_chip)),
            "newton_rest",
            jax.ShapeDtypeStruct(chip.shape, bf16),
            [VMEM] * (1 + len(to_chip)),
            VMEM,
            (chip, *cross(chip.astype(bf16))),
        )
        turned = call(
            functools.partial(turn_rest_kernel, CORES * cap, entries - 1),
            "turn_rest",
            pltpu.HBM(turned.shape, bf16),
            [SMEM] * 3 + [VMEM] * 3 + [HBM] * 2,
            HBM,
            (block_list, lengths, table[0, :entries], own, swap(own), centroids, stay(points), stay(turned)),
            scratch=[pltpu.VMEM((rows, width), bf16)],
            aliases={7: 0},
        )
        return turned

    return lax.cond(overflow, exchange_rest, lambda state: state[0], (turned, rest_chip))


def solution(mesh):
    return jax.shard_map(
        functools.partial(local, mesh.shape["wide"], mesh.shape["narrow"]),
        mesh=mesh,
        in_specs=(
            P("wide", "narrow", None),
            P("wide", "narrow", None),
            P("wide", None),
            P("wide"),
            P("wide"),
            P("wide"),
        ),
        out_specs=P("wide", "narrow", None),
        check_vma=False,
    )
```

```python
import functools

import jax
import jax.numpy as jnp
from jax import lax
from jax.experimental import pallas as pl
from jax.experimental.pallas import tpu as pltpu
from jax.sharding import PartitionSpec as P

MOVE = 2
ITERS = 5
CORES = 2
PIECES = 2
STORES = 8
VMEM_LIMIT = 14 * 1024 * 1024
LONG = 1 << 30
GROUP = 4
LEAD_FLOPS = 600000000
PAIR_FLOPS = 1500000000

f32, bf16, i32 = jnp.float32, jnp.bfloat16, jnp.int32

SMEM = pl.BlockSpec(memory_space=pltpu.SMEM)
VMEM = pl.BlockSpec(memory_space=pltpu.VMEM)
HBM = pl.BlockSpec(memory_space=pltpu.HBM)
ANY = pl.BlockSpec(memory_space=pl.ANY)


def stay(x):
    return pltpu.with_memory_space_constraint(x, pltpu.HBM)


def call(kernel, name, outs, in_specs, out_specs, args, moved=1 << 20, flops=0, scratch=(), aliases={}):
    return pl.pallas_call(
        kernel,
        out_shape=outs,
        in_specs=in_specs,
        out_specs=out_specs,
        scratch_shapes=scratch,
        input_output_aliases=aliases,
        compiler_params=pltpu.CompilerParams(vmem_limit_bytes=VMEM_LIMIT),
        cost_estimate=pl.CostEstimate(flops=16 * moved if moved == LONG else flops, bytes_accessed=moved, transcendentals=0),
        name=name,
    )(*args)


def assign_slots(bl, ln, first_rows, slot_of_list, plan):
    blocks, lists = bl.shape[0], slot_of_list.shape[0]
    for l in range(lists):
        slot_of_list[l] = -1

    def visit(b, nxt, wanted):
        l = bl[b]
        s = slot_of_list[l]
        new = jnp.logical_and(s < 0, wanted)
        slot_of_list[l] = jnp.where(new, nxt, s)
        return nxt + new.astype(i32)

    nxt = jnp.int32(0)
    for b in range(MOVE):
        nxt = visit(b, nxt, True)
    for b in range(MOVE, blocks):
        nxt = visit(b, nxt, ln[b] > first_rows)
    plan[blocks + 1 + MOVE] = nxt
    for b in range(MOVE, blocks):
        nxt = visit(b, nxt, True)
    plan[blocks] = nxt
    for b in range(blocks):
        plan[b] = slot_of_list[bl[b]]


def gram_kernel(bl_hbm, ln_hbm, sources_hbm, points_hbm, targets_hbm, centroids_hbm, table, residual, same, acc, send, *scratch):
    bl, ln, sources, slot_of_list, plan, points, targets, centroids, sems, int_sems = scratch
    blocks, rows, _ = points.shape
    per = acc.shape[0] // CORES
    piece = blocks // PIECES
    copies = [
        pltpu.make_async_copy(bl_hbm, bl, int_sems.at[0]),
        pltpu.make_async_copy(ln_hbm, ln, int_sems.at[1]),
        pltpu.make_async_copy(centroids_hbm, centroids, int_sems.at[2]),
        pltpu.make_async_copy(sources_hbm, sources, int_sems.at[3]),
    ]
    for copy in copies:
        copy.start()
    parts = []
    for i in range(PIECES):
        at = pl.ds(i * piece, piece)
        pair = (
            pltpu.make_async_copy(points_hbm.at[at], points.at[at], sems.at[0, i]),
            pltpu.make_async_copy(targets_hbm.at[at], targets.at[at], sems.at[1, i]),
        )
        for copy in pair:
            copy.start()
        parts.append(pair)
    me = lax.axis_index("narrow")
    core = lax.rem(me, CORES)
    acc[...] = jnp.zeros_like(acc)
    copies[0].wait()
    copies[1].wait()
    assign_slots(bl, ln, CORES * rows, slot_of_list, plan)
    copies[2].wait()
    copies[3].wait()
    for j in range(MOVE):
        plan[blocks + 1 + j] = lax.div(sources[j], blocks)
        mine = lax.rem(plan[j], CORES) == core
        same[j] = jnp.full(same.shape[1:], jnp.where(mine, 1.0, 0.0), f32)
    lanes = lax.broadcasted_iota(i32, table.shape, 1)
    entries = jnp.zeros(table.shape, i32)
    for k in range(plan.shape[0]):
        entries = jnp.where(lanes == k, plan[k], entries)
    table[...] = entries
    row_ids = lax.broadcasted_iota(i32, points.shape[1:], 0) + me * rows
    for i in range(PIECES):
        for copy in parts[i]:
            copy.wait()
        for b in range(i * piece, (i + 1) * piece):
            kept = row_ids < ln[b]
            res = jnp.where(kept, points[b].astype(f32) - centroids[pl.ds(bl[b], 1), :], 0.0).astype(bf16)
            residual[b] = res
            slot = plan[b]
            at = lax.div(slot, CORES) + jnp.where(lax.rem(slot, CORES) == core, 0, per)
            acc[at] += lax.dot_general(res, targets[b], (((0,), (0,)), ((), ())), preferred_element_type=f32)
    for i in range(send.shape[0]):
        send[i] = acc[per + i].astype(bf16)


def lead_sum_kernel(per, acc, recv, chip, *sends):
    at = chip.shape[0]
    chip[...] = (acc[:at] + recv[...].astype(f32)).astype(bf16)
    for out in sends:
        count = out.shape[0]
        out[...] = acc[per + at:per + at + count].astype(bf16)
        at += count


def table_kernel(table, _, out):
    out[...] = table[...]


def sum_kernel(first, acc, recv, *refs):
    out = refs[-1]
    count = out.shape[0]
    out[...] = (acc[first:first + count] + recv[...].astype(f32)).astype(bf16)


def newton_kernel(count, first, offset, extra, keep, acc, recv, *refs):
    pieces, out, chip = refs[:-2], refs[-2], refs[-1]
    grams = []
    for i in range(count):
        g = acc[first + i] + recv[offset + i].astype(f32)
        if keep:
            chip[i] = g
        for which in extra:
            piece, row = which[i]
            g = g + pieces[piece][row].astype(f32)
        grams.append(g)
    polar(grams, out)


def polar(grams, out):
    xs = []
    for g in grams:
        gb = g.astype(bf16)
        p = lax.dot_general(gb, gb, (((1,), (1,)), ((), ())), preferred_element_type=f32)
        scale = lax.rsqrt(jnp.sum(g * g) + 1e-6)
        p = (p * (scale * scale)).astype(bf16)
        xs.append((1.5 * scale) * g - (0.5 * scale) * jnp.dot(p, gb, preferred_element_type=f32))
    for _ in range(ITERS - 1):
        for i, x in enumerate(xs):
            xb = x.astype(bf16)
            p = lax.dot_general(xb, xb, (((1,), (1,)), ((), ())), preferred_element_type=f32).astype(bf16)
            xs[i] = 1.5 * x - 0.5 * jnp.dot(p, xb, preferred_element_type=f32)
    for i, x in enumerate(xs):
        out[i] = x.astype(bf16)


def newton(acc, first, count, recv, offset, crossed, after=(), keep=False, moved=1 << 20):
    extra = [[] for _ in (crossed[0] if crossed else ())]
    flat = []
    for group in crossed:
        for chip, part in enumerate(group):
            extra[chip] += [(len(flat), row) for row in range(part.shape[0])]
            flat.append(part)
    shape = (count,) + acc.shape[1:]
    out = call(
        functools.partial(newton_kernel, count, first, offset, extra, keep),
        "newton",
        (jax.ShapeDtypeStruct(shape, bf16),) + ((jax.ShapeDtypeStruct(shape, f32),) if keep else ()),
        [VMEM] * (2 + len(flat)) + [ANY] * len(after),
        (VMEM,) * (1 + keep),
        (acc, recv, *flat, *after),
        moved=moved,
        scratch=[] if keep else [pltpu.VMEM((8, 128), f32)],
    )
    return out if keep else out[0]


def newton_rest_kernel(others, chip, *refs):
    out = refs[-1]
    grams = []
    for i in range(chip.shape[0]):
        g = chip[i]
        for other in refs[:others]:
            g = g + other[i].astype(f32)
        grams.append(g)
    polar(grams, out)


def leading_kernel(same, residual, own, sibling, out):
    for b in range(MOVE):
        rotation = jnp.where(same[b, :1] > 0.5, own[0], sibling[0])
        out[b] = jnp.dot(residual[b], rotation, preferred_element_type=f32).astype(bf16)


def pair_kernel(near, far, *refs):
    out = refs[-1]
    out[0] = near[...]
    out[1] = far[...]


def arrived_kernel(*refs):
    refs[-1][...] = jnp.zeros_like(refs[-1])


def gather_kernel(starts, n_own, *refs):
    owns, siblings, rots = refs[:n_own], refs[n_own:-1], refs[-1]
    core = lax.rem(lax.axis_index("narrow"), CORES)
    for s, own in zip(starts, owns):
        for i in range(own.shape[0]):
            rots[CORES * (s + i) + core] = own[i]
    for s, sibling in zip(starts, siblings):
        for i in range(sibling.shape[0]):
            rots[CORES * (s + i) + 1 - core] = sibling[i]


def turn_kernel(first, hops, table, residual, main, _, *refs):
    parts = refs[:len(hops)]
    out, rots, turned, sems = refs[-4:]
    blocks, rows, _ = residual.shape
    piece = blocks // STORES
    core = lax.rem(lax.axis_index("narrow"), CORES)
    here = lax.axis_index("wide")
    plan = table[...]
    for i in range(main.shape[0]):
        rots[CORES * (first + i) + 1 - core] = main[i]
    copies = []
    for i in reversed(range(STORES)):
        for b in reversed(range(i * piece, (i + 1) * piece)):
            if b >= MOVE:
                turned[b] = jnp.dot(residual[b], rots[plan[0, b]], preferred_element_type=f32).astype(bf16)
                continue
            donor = plan[0, blocks + 1 + b]
            picked = parts[0][0, b]
            for part, group in zip(parts, hops):
                for k, hop in enumerate(group):
                    match = donor == (hop if len(parts) == 1 else here ^ hop)
                    picked = jnp.where(match, part[k, b], picked)
            turned[b] = picked
        at = pl.ds(i * piece, piece)
        copies.append(pltpu.make_async_copy(turned.at[at], out.at[at], sems.at[i]))
        copies[-1].start()
    for copy in copies:
        copy.wait()


def turn_rest_kernel(first, last, bl, ln, plan, own, sibling, centroids, points_hbm, _, out, block):
    blocks, rows, _ = points_hbm.shape
    me = lax.axis_index("narrow")
    core = lax.rem(me, CORES)
    row_ids = lax.broadcasted_iota(i32, block.shape, 0) + me * rows

    @pl.loop(MOVE, blocks)
    def _(b):
        @pl.when(jnp.logical_and(plan[b] >= first, plan[b] < plan[last]))
        def _():
            pltpu.sync_copy(points_hbm.at[b], block)
            kept = row_ids < ln[b]
            residual = jnp.where(kept, block[...].astype(f32) - centroids[pl.ds(bl[b], 1), :], 0.0).astype(bf16)
            at = lax.div(plan[b] - first, CORES)
            mine = lax.rem(plan[b], CORES) == core
            rotation = jnp.where(mine, own[at], sibling[at])
            block[...] = jnp.dot(residual, rotation, preferred_element_type=f32).astype(bf16)
            pltpu.sync_copy(block, out.at[b])


def local(wide, narrow, points, targets, centroids, block_list, lengths, sources):
    blocks, rows, width = points.shape
    lists = centroids.shape[0]
    per = lists // CORES
    chips = narrow // CORES
    mat = (width, width)
    lead = MOVE // CORES
    cap = per * 3 // 4 if chips == 2 else per
    rest = per - cap

    entries = blocks + 2 + MOVE
    table, residual, same, acc, send = call(
        gram_kernel,
        "grams",
        (
            jax.ShapeDtypeStruct((8, -(-entries // 128) * 128), i32),
            jax.ShapeDtypeStruct(points.shape, bf16),
            jax.ShapeDtypeStruct((MOVE, 8, width), f32),
            jax.ShapeDtypeStruct((lists,) + mat, f32),
            jax.ShapeDtypeStruct((lead,) + mat, bf16),
        ),
        [HBM] * 6,
        (VMEM,) * 5,
        tuple(stay(x) for x in (block_list, lengths, sources, points, targets, centroids)),
        scratch=[
            pltpu.SMEM((blocks,), i32),
            pltpu.SMEM((blocks,), i32),
            pltpu.SMEM((blocks,), i32),
            pltpu.SMEM((lists,), i32),
            pltpu.SMEM((entries,), i32),
            pltpu.VMEM(points.shape, bf16),
            pltpu.VMEM(points.shape, bf16),
            pltpu.VMEM(centroids.shape, f32),
            pltpu.SemaphoreType.DMA((2, PIECES)),
            pltpu.SemaphoreType.DMA((4,)),
        ],
    )

    to_core = [(i, i ^ 1) for i in range(narrow)]
    to_chip = [[(i, (i + CORES * k) % narrow) for i in range(narrow)] for k in range(1, chips)]

    def cross(part):
        return tuple(lax.ppermute(part, "narrow", perm) for perm in to_chip)

    def swap(part):
        return lax.ppermute(part, "narrow", to_core)

    recv = swap(send)
    counts = (lead, cap - lead) + (rest,) * (rest > 0)
    lead_chip, *sends = call(
        functools.partial(lead_sum_kernel, per),
        "lead_sum",
        tuple(jax.ShapeDtypeStruct((count,) + mat, bf16) for count in counts),
        [VMEM, VMEM],
        (VMEM,) * len(counts),
        (acc, recv),
    )
    lead_crossed = cross(lead_chip)
    recv_main = swap(sends[0])
    after = ()
    if rest:
        late_table = call(
            table_kernel,
            "table",
            jax.ShapeDtypeStruct(table.shape, i32),
            [VMEM, ANY],
            VMEM,
            (table, recv_main),
        )
        overflow = late_table[0, entries - 1] > CORES * cap
        after = (overflow.astype(i32).reshape(1),)
    main_chip = call(
        functools.partial(sum_kernel, lead),
        "main_sum",
        jax.ShapeDtypeStruct((cap - lead,) + mat, bf16),
        [VMEM, VMEM] + [ANY] * len(after),
        VMEM,
        (acc, recv_main, *after),
    )
    main_crossed = cross(main_chip)
    owns = [newton(acc, 0, lead, recv, 0, (lead_crossed,), (main_chip,))]
    siblings = [swap(owns[0])]

    leading = call(
        leading_kernel,
        "turn_leading",
        jax.ShapeDtypeStruct((MOVE, rows, width), bf16),
        [VMEM] * 4,
        VMEM,
        (same, residual, owns[0], siblings[0]),
        flops=LEAD_FLOPS,
    )
    starts, tokens = [0], ()
    if rest:
        starts.append(cap)
        rest_own, rest_chip = newton(acc, cap, rest, swap(sends[1]), 0, (), (leading,), True, 1 << 12)
        owns.append(rest_own)
        tokens = (rest_own,)
    if wide <= 16 and wide & (wide - 1) == 0:
        half = wide // 2
        far = lax.ppermute(leading, "wide", [(i, i ^ half) for i in range(wide)])
        pair = call(
            pair_kernel,
            "pair",
            jax.ShapeDtypeStruct((2,) + leading.shape, bf16),
            [VMEM, VMEM] + [ANY] * len(tokens),
            VMEM,
            (leading, far, *tokens),
            flops=PAIR_FLOPS,
        )
        order = (half - 1, *range(1, half - 1))
        parts = [pair] + [lax.ppermute(pair, "wide", [(i, i ^ k) for i in range(wide)]) for k in order]
        hops = [(k, k ^ half) for k in [0, *order]]
        token = pair
    else:
        parts = [lax.all_gather(leading, "wide", axis=0)]
        hops = [tuple(range(wide))]
        token = leading
    main = newton(acc, lead, cap - lead, recv_main, 0, (main_crossed,), (token,))
    siblings += [swap(own) for own in owns[1:]]
    other = swap(main)

    rots = call(
        functools.partial(gather_kernel, starts + [lead], len(owns) + 1),
        "gather_rotations",
        jax.ShapeDtypeStruct((lists,) + mat, bf16),
        [VMEM] * (1 + len(owns) + len(siblings)),
        VMEM,
        (*owns, main, *siblings),
    )
    token = call(
        arrived_kernel,
        "arrived",
        jax.ShapeDtypeStruct((8, 128), f32),
        [ANY] * (1 + len(parts)),
        VMEM,
        (*parts, rots),
        moved=LONG,
    )
    turned, _ = call(
        functools.partial(turn_kernel, lead, hops),
        "turn",
        (pltpu.HBM(points.shape, bf16), jax.ShapeDtypeStruct(rots.shape, bf16)),
        [VMEM] * (4 + len(parts)) + [ANY],
        (HBM, VMEM),
        (table, residual, other, rots, *parts, token),
        scratch=[
            pltpu.VMEM(points.shape, bf16),
            pltpu.SemaphoreType.DMA((STORES,)),
        ],
        aliases={3: 1},
    )
    if not rest:
        return turned

    def exchange_rest(state):
        turned, chip = state
        own = call(
            functools.partial(newton_rest_kernel, len(to_chip)),
            "newton_rest",
            jax.ShapeDtypeStruct(chip.shape, bf16),
            [VMEM] * (1 + len(to_chip)),
            VMEM,
            (chip, *cross(chip.astype(bf16))),
        )
        turned = call(
            functools.partial(turn_rest_kernel, CORES * cap, entries - 1),
            "turn_rest",
            pltpu.HBM(turned.shape, bf16),
            [SMEM] * 3 + [VMEM] * 3 + [HBM] * 2,
            HBM,
            (block_list, lengths, table[0, :entries], own, swap(own), centroids, stay(points), stay(turned)),
            scratch=[pltpu.VMEM((rows, width), bf16)],
            aliases={7: 0},
        )
        return turned

    return lax.cond(overflow, exchange_rest, lambda state: state[0], (turned, rest_chip))


def solution(mesh):
    return jax.shard_map(
        functools.partial(local, mesh.shape["wide"], mesh.shape["narrow"]),
        mesh=mesh,
        in_specs=(
            P("wide", "narrow", None),
            P("wide", "narrow", None),
            P("wide", None),
            P("wide"),
            P("wide"),
            P("wide"),
        ),
        out_specs=P("wide", "narrow", None),
        check_vma=False,
    )
```
